128 devices in a mesh: rows: 16 (over y, z), feat: 8 (over x, core).
Axes of the slice: x: 4, y: 4, z: 4, core: 2. Of those that a mesh axis runs over, the one named last changes fastest.
Arguments:
- features: float32 [65536, 8192], P('rows', 'feat'), may hold values from -0.0234375 to 0.0234375
- targets: float32 [32, 65536], P(None, 'rows'), may hold values from -6 to 6
- counts: int32 [16], P('rows'), may hold values from 1 to 4096, as said below
- ranks: int32 [65536], P('rows'), may hold values from 1 to 65536
Outputs:
- solution: float32 [32, 8192], P(None, 'feat')
- residual: float32 [32, 8192], P(None, 'feat')
The draws below stay inside these ranges and needn't reach their ends.
Inputs may be any that keep to these rules, and one draw needn't show every extreme that they name: `counts`: one shard in every draw holds all 4096 slots live.
All inputs are finite; a program needn't handle non-finite values.
Results may differ from the reference program's by a relative error of at most 0.0003.
Values sent between devices are 32-bit elements; how exact they have to be, the bound alone decides.
No kernel may reach another device: no remote copies, remote signals or barrier semaphores. Data moves between devices by JAX's collectives and lax.ppermute only.
A program may use at most 64 MiB of HBM per device.

```python
import jax
import jax.numpy as jnp
from jax import lax

F = 8192
K = 32
CAP = 4096
ITERS = 2
SHARDS = 16
TOTAL = 65536


def draw_counts(key, part):
    key = jax.random.fold_in(key, 5)
    jitter_key = jax.random.fold_in(key, 1)
    order_key = jax.random.fold_in(key, 2)
    shard_ids = jnp.arange(SHARDS, dtype=jnp.int32)
    low_count = CAP // 3
    ramp_counts = low_count + (CAP - low_count) * shard_ids // max(SHARDS - 1, 1)
    jitter = jax.random.randint(jitter_key, (SHARDS,), 0, CAP // 8 + 1, dtype=jnp.int32)
    ordered = jnp.where(shard_ids == SHARDS - 1, CAP, ramp_counts - jitter)
    shuffle = jax.random.permutation(order_key, SHARDS)
    return ordered[shuffle].astype(jnp.int32)


def place_ends(array, key, smallest, largest):
    index_at = [jax.random.randint(jax.random.fold_in(key, axis), (), 0, length) for axis, length in enumerate(array.shape)]
    main_axis = array.shape.index(max(array.shape))
    beside = index_at[:main_axis] + [(index_at[main_axis] + 1) % array.shape[main_axis]] + index_at[main_axis + 1:]
    return array.at[tuple(index_at)].set(smallest).at[tuple(beside)].set(largest)


def levels(stream_key, shape, split, low, largest):
    def one(position, shards_of):
        heights = jax.random.uniform(jax.random.fold_in(jax.random.fold_in(stream_key, 6), position), (shards_of,), jnp.float32, low / len(split), largest / len(split))
        return jnp.repeat(jnp.exp(heights), shape[position] // shards_of).reshape((-1,) + (1,) * (len(shape) - position - 1))

    factor_of = one(*split[0])
    for cut in split[1:]:
        factor_of = factor_of * one(*cut)
    return factor_of


def scatter_about(own_key, extent, deviation, limit, pieces=(), kind=jnp.bfloat16):
    values = jax.random.normal(own_key, extent, jnp.float32) * deviation
    if len(pieces) > 0:
        values = levels(own_key, extent, pieces, -0.22, 0.18) * values
    return jnp.clip(values, min=-limit, max=limit).astype(kind)


def setup_inputs(seed: int = 0) -> dict:
    streams_of = jax.random.split(jax.random.key(seed), 5)
    return {
        "features": scatter_about(streams_of[0], (TOTAL, F), TOTAL ** -0.5, 0.0234375, ((0, 16), (1, 8)), jnp.float32),
        "targets": scatter_about(streams_of[1], (K, TOTAL), 1.0, 6.0, ((1, 16),), jnp.float32),
        "counts": draw_counts(jax.random.fold_in(streams_of[4], 71), 0),
        "ranks": place_ends(jax.random.randint(streams_of[3], (TOTAL,), 1, TOTAL + 1), jax.random.fold_in(streams_of[3], 1), 1, TOTAL).astype(jnp.int32),
    }


prio_power = 0.7
weight_power = 0.5
ridge_shift = 0.5

def spd_solve(matrix, rhs_block):
    matrix = 0.5 * (matrix + matrix.T)
    lower = jnp.linalg.cholesky(matrix)
    return jax.scipy.linalg.cho_solve((lower, True), rhs_block)

def reference(features, targets, counts, ranks):
    highest = lax.Precision.HIGHEST
    row_index = jnp.arange(TOTAL, dtype=jnp.int32) % CAP
    live_row = row_index < jnp.repeat(counts, CAP)
    raw_prio = ranks.astype(jnp.float32) ** (-prio_power)
    priority = jnp.where(live_row, raw_prio, 0.0)
    total_prio = jnp.sum(priority)
    live_total = jnp.sum(counts).astype(jnp.float32)
    weights = jnp.where(live_row, (live_total * raw_prio / total_prio) ** (-weight_power), 0.0)
    rhs_field = jnp.dot(targets * weights[None, :], features, precision=highest)
    solution = jnp.zeros_like(rhs_field)
    residual = rhs_field
    direction = rhs_field
    gram_now = jnp.dot(residual, residual.T, precision=highest)
    for iteration in range(ITERS):
        images = lax.dot_general(direction, features, (((1,), (1,)), ((), ())), precision=highest)
        backward = jnp.dot(images * weights[None, :], features, precision=highest) + ridge_shift * direction
        curvature = jnp.dot(direction, backward.T, precision=highest)
        step_size = spd_solve(curvature, gram_now)
        solution = solution + jnp.dot(step_size.T, direction, precision=highest)
        residual = residual - jnp.dot(step_size.T, backward, precision=highest)
        if iteration + 1 < ITERS:
            gram_new = jnp.dot(residual, residual.T, precision=highest)
            conj_coef = spd_solve(gram_now, gram_new)
            direction = residual + jnp.dot(conj_coef.T, direction, precision=highest)
            gram_now = gram_new
    return (solution, residual)
```

```python
import functools

import jax
import jax.numpy as jnp
from jax import lax
from jax.experimental import pallas as pl
from jax.experimental.pallas import tpu as pltpu
from jax.sharding import PartitionSpec as P


K = 32
HALF = K // 2
EXTRA = 128
XCHIPS = 4
CHUNK = 512
BUFFERS = 4
prio_power = 0.7
weight_power = 0.5
ridge_shift = 0.5
f32, bf16 = jnp.float32, jnp.bfloat16
IN_VMEM = pl.BlockSpec(memory_space=pltpu.VMEM)
IN_SMEM = pl.BlockSpec(memory_space=pltpu.SMEM)
ANYWHERE = pl.BlockSpec(memory_space=pl.ANY)
ROWS_BY_ROWS = (((1,), (1,)), ((), ()))


def split(value):
    high = value.astype(bf16)
    return high, (value - high.astype(f32)).astype(bf16)


def exact(left, right):
    return jnp.dot(left, right, precision=lax.Precision.HIGHEST, preferred_element_type=f32)


def row_gram(left, right):
    return lax.dot_general(left, right, ROWS_BY_ROWS, precision=lax.Precision.HIGHEST, preferred_element_type=f32)


def solve_t(matrix, rhs_block):
    matrix = 0.5 * (matrix + matrix.T)
    table = jnp.concatenate([matrix, rhs_block], axis=1)
    row_id = lax.broadcasted_iota(jnp.int32, (K, 1), 0)
    for k in range(K):
        row = table[k : k + 1, :] / table[k : k + 1, k : k + 1]
        table = jnp.where(row_id == k, row, table - table[:, k : k + 1] * row)
    return table[:, K:].T


def merged(parts):
    a, b, c, d = (part[...] for part in parts)
    return (a + b) + (c + d)


def k1(count, ranks_any, targets_any, features, high, low, scale, out, buf, targets, ranks, pair, sem, in_sem):
    slots, width = features.shape
    steps = slots // CHUNK
    small = [
        pltpu.make_async_copy(ranks_any, ranks, in_sem.at[0]),
        pltpu.make_async_copy(targets_any, targets, in_sem.at[1]),
    ]
    copies = [
        pltpu.make_async_copy(features.at[pl.ds(c * CHUNK, CHUNK)], buf.at[c % BUFFERS], sem.at[c % BUFFERS])
        for c in range(steps)
    ]
    for copy in small:
        copy.start()
    for c in range(BUFFERS):
        copies[c].start()
    live = lax.broadcasted_iota(jnp.int32, (1, slots), 1) < count[0]
    small[0].wait()
    log_rank = jnp.log(ranks[...].astype(f32))
    scale_now = jnp.where(live, jnp.exp((prio_power * weight_power) * log_rank), 0.0)
    scale[...] = scale_now
    prio_sum = jnp.sum(jnp.where(live, jnp.exp(-prio_power * log_rank), 0.0))
    small[1].wait()
    high_t, low_t = split(targets[...] * scale_now)
    pair[0:K, :] = high_t
    pair[K : 2 * K, :] = low_t
    total = jnp.zeros((2 * K, width), f32)
    rest = jnp.zeros((K, width), f32)
    for c in range(steps):
        at = slice(c * CHUNK, (c + 1) * CHUNK)
        copies[c].wait()
        high_f, low_f = split(buf[c % BUFFERS])
        if c + BUFFERS < steps:
            copies[c + BUFFERS].start()
        high[at, :] = high_f
        low[at, :] = low_f
        total += jnp.dot(pair[:, at], high_f, preferred_element_type=f32)
        rest += jnp.dot(pair[0:K, at], low_f, preferred_element_type=f32)
    out[:, 0:width] = total[0:K] + total[K:] + rest
    row = lax.broadcasted_iota(jnp.int32, (K, EXTRA), 0)
    col = lax.broadcasted_iota(jnp.int32, (K, EXTRA), 1)
    tail = jnp.where(col == 0, prio_sum, jnp.where(col == 1, count[0].astype(f32), 0.0))
    out[:, width:] = jnp.where(row == 0, tail, 0.0)


def put_images(field, gram, high, low, mine, other):
    place = lax.axis_index("feat")
    x, first = place // 2, place % 2 == 0
    slots = high.shape[0]
    part = slots // XCHIPS
    high_v, low_v = split(field)
    pair = jnp.concatenate([high_v, low_v], axis=0)
    blank = jnp.zeros((K, EXTRA - gram.shape[1]), f32)
    gram = jnp.concatenate([gram, blank], axis=1)
    for c in range(XCHIPS):
        slot = x ^ c
        for piece in range(part // CHUNK):
            at = slice(c * part + piece * CHUNK, c * part + (piece + 1) * CHUNK)
            to = slice(piece * CHUNK, (piece + 1) * CHUNK)
            both = lax.dot_general(pair, high[at, :], ROWS_BY_ROWS, preferred_element_type=f32)
            rest = lax.dot_general(high_v, low[at, :], ROWS_BY_ROWS, preferred_element_type=f32)
            value = both[0:K] + both[K:] + rest
            mine[slot, :, to] = jnp.where(first, value[0:HALF], value[HALF:])
            other[slot, :, to] = jnp.where(first, value[HALF:], value[0:HALF])
        tail = gram if c == 0 else jnp.zeros_like(gram)
        mine[slot, :, part:] = jnp.where(first, tail[0:HALF], tail[HALF:])
        other[slot, :, part:] = jnp.where(first, tail[HALF:], tail[0:HALF])


def k2(p0, p1, p2, p3, high, low, field, norm, mine, other):
    width = high.shape[1]
    total = merged((p0, p1, p2, p3))
    factor = jnp.sqrt(total[0:1, width : width + 1] / total[0:1, width + 1 : width + 2])
    norm[...] = jnp.broadcast_to(factor, norm.shape)
    rhs_field = total[:, 0:width] * factor
    field[...] = rhs_field
    put_images(rhs_field, row_gram(rhs_field, rhs_field), high, low, mine, other)


def get_images(near, far):
    first = lax.axis_index("feat") % 2 == 0
    out = []
    for j, ref in enumerate(near):
        a, b = ref[...], far[j]
        out.append(jnp.concatenate([jnp.where(first, a, b), jnp.where(first, b, a)], axis=0))
    return out


def owned(chunks, part):
    x = lax.axis_index("feat") // 2
    tail = chunks[0][:, part:]
    for j in range(1, XCHIPS):
        tail = jnp.where(x == j, chunks[j][:, part:], tail)
    return tail


def back_project(images, scale, high, low, out):
    x = lax.axis_index("feat") // 2
    part, width = images[0].shape[1], high.shape[1]
    total = jnp.zeros((2 * K, width), f32)
    rest = jnp.zeros((K, width), f32)
    curve = jnp.zeros((2 * K, 2 * K), f32)
    for j in range(XCHIPS):
        base = pl.multiple_of((x ^ j) * part, part)
        weighted = images[j] * scale[:, pl.ds(base, part)]
        high_w, low_w = split(weighted)
        high_i, low_i = split(images[j])
        pair = jnp.concatenate([high_w, low_w], axis=0)
        curve += lax.dot_general(pair, jnp.concatenate([high_i, low_i], axis=0), ROWS_BY_ROWS, preferred_element_type=f32)
        for piece in range(part // CHUNK):
            at = pl.ds(pl.multiple_of(base + piece * CHUNK, CHUNK), CHUNK)
            to = slice(piece * CHUNK, (piece + 1) * CHUNK)
            total += jnp.dot(pair[:, to], high[at, :], preferred_element_type=f32)
            rest += jnp.dot(high_w[:, to], low[at, :], preferred_element_type=f32)
    out[:, 0:width] = total[0:K] + total[K:] + rest
    curve = curve[0:K, 0:K] + curve[0:K, K:] + curve[K:, 0:K]
    out[:, width:] = jnp.concatenate([curve, jnp.zeros((K, EXTRA - K), f32)], axis=1)


def k3(n0, n1, n2, n3, far, scale, high, low, out, kept, gram):
    part = kept.shape[2]
    chunks = get_images((n0, n1, n2, n3), far)
    gram[...] = owned(chunks, part)[:, 0:K]
    images = [chunk[:, 0:part] for chunk in chunks]
    for j in range(XCHIPS):
        kept[j] = images[j]
    back_project(images, scale, high, low, out)


def k4(z0, z1, z2, z3, field, norm, gram, high, low, residual, step, mine, other):
    width = high.shape[1]
    total = merged((z0, z1, z2, z3)) * norm[0:1, 0:1]
    backward = total[:, 0:width] + ridge_shift * field[...]
    curvature = total[:, width : width + K] + ridge_shift * gram[...]
    step_t = solve_t(curvature, gram[...])
    step[...] = step_t
    now = field[...] - exact(step_t, backward)
    residual[...] = now
    grams = jnp.concatenate([row_gram(now, now), row_gram(now, field[...])], axis=1)
    put_images(now, grams, high, low, mine, other)


def k5(n0, n1, n2, n3, far, kept, gram, scale, high, low, out, coef, grams):
    part = kept.shape[2]
    chunks = get_images((n0, n1, n2, n3), far)
    tail = owned(chunks, part)
    grams[...] = tail[:, 0 : 2 * K]
    coef_t = solve_t(gram[...], tail[:, 0:K])
    coef[...] = coef_t
    images = [chunk[:, 0:part] + exact(coef_t, kept[j]) for j, chunk in enumerate(chunks)]
    back_project(images, scale, high, low, out)


def k6(z0, z1, z2, z3, field, residual, norm, gram, grams, step, coef, solution_out, residual_out):
    width = field.shape[1]
    coef_t = coef[...]
    gram_new, cross = grams[:, 0:K], grams[:, K : 2 * K]
    mixed = row_gram(cross, coef_t)
    square = gram_new + mixed + mixed.T + row_gram(exact(coef_t, gram[...]), coef_t)
    total = merged((z0, z1, z2, z3)) * norm[0:1, 0:1]
    direction = residual[...] + exact(coef_t, field[...])
    backward = total[:, 0:width] + ridge_shift * direction
    curvature = total[:, width : width + K] + ridge_shift * square
    step_t = solve_t(curvature, gram_new)
    solution_out[...] = exact(step[...], field[...]) + exact(step_t, direction)
    residual_out[...] = residual[...] - exact(step_t, backward)


def call(kernel, outs, operands, specs=None, scratch=(), limit=24):
    return pl.pallas_call(
        kernel,
        out_shape=outs,
        in_specs=specs or [IN_VMEM] * len(operands),
        out_specs=[IN_VMEM] * len(outs),
        scratch_shapes=scratch,
        compiler_params=pltpu.CompilerParams(vmem_limit_bytes=limit << 20),
        name=kernel.__name__,
    )(*operands)


def exchange(value, axis, size, distance):
    return lax.ppermute(value, axis, [(i, i ^ distance) for i in range(size)])


def gather_rows(value):
    near = [value] + [exchange(value, "rows", 16, d) for d in (1, 2, 3)]
    value = (near[0] + near[1]) + (near[2] + near[3])
    return [value] + [exchange(value, "rows", 16, d) for d in (4, 8, 12)]


def sum_feat(mine, other):
    value = mine + exchange(other, "feat", 8, 1)
    got = [value[0]] + [exchange(value[j], "feat", 8, 2 * j) for j in (1, 2, 3)]
    value = (got[0] + got[1]) + (got[2] + got[3])
    near = [value] + [exchange(value, "feat", 8, 2 * j) for j in (1, 2, 3)]
    far = exchange(jnp.stack(near), "feat", 8, 1)
    return [*near, far]


def local(features, targets, counts, ranks):
    slots, width = features.shape
    part = slots // XCHIPS
    shape = jax.ShapeDtypeStruct
    summed = shape((K, width + EXTRA), f32)
    field_like, small = shape((K, width), f32), shape((K, K), f32)
    images_like = [shape((XCHIPS, HALF, part + EXTRA), f32)] * 2
    high, low, scale, out = call(
        k1,
        [pltpu.VMEM((slots, width), bf16), pltpu.VMEM((slots, width), bf16), shape((1, slots), f32), summed],
        (counts, ranks.reshape(1, slots), targets, features),
        [IN_SMEM, ANYWHERE, ANYWHERE, ANYWHERE],
        (
            pltpu.VMEM((BUFFERS, CHUNK, width), f32),
            pltpu.VMEM((K, slots), f32),
            pltpu.VMEM((1, slots), jnp.int32),
            pltpu.VMEM((2 * K, slots), bf16),
            pltpu.SemaphoreType.DMA((BUFFERS,)),
            pltpu.SemaphoreType.DMA((2,)),
        ),
    )
    parts = gather_rows(out)
    field, norm, mine, other = call(k2, [field_like, shape((8, 128), f32), *images_like], (*parts, high, low))
    parts = sum_feat(mine, other)
    out, kept, gram = call(
        k3, [summed, shape((XCHIPS, K, part), f32), small], (*parts, scale, high, low)
    )
    parts = gather_rows(out)
    residual, step, mine, other = call(
        k4, [field_like, small, *images_like], (*parts, field, norm, gram, high, low)
    )
    parts = sum_feat(mine, other)
    out, coef, grams = call(
        k5, [summed, small, shape((K, 2 * K), f32)], (*parts, kept, gram, scale, high, low)
    )
    parts = gather_rows(out)
    return tuple(
        call(k6, [field_like, field_like], (*parts, field, residual, norm, gram, grams, step, coef))
    )


def solution(mesh):
    placed = (P("rows", "feat"), P(None, "rows"), P("rows"), P("rows"))
    return jax.shard_map(
        local,
        mesh=mesh,
        in_specs=placed,
        out_specs=(P(None, "feat"), P(None, "feat")),
        check_vma=False,
    )
```

```python
import jax
import jax.numpy as jnp
from jax import lax
from jax.experimental import pallas as pl
from jax.experimental.pallas import tpu as pltpu
from jax.sharding import PartitionSpec as P


K = 32
HALF = K // 2
LANES = 128
TILE = 8
XCHIPS = 4
DISTANCES = (0, 1, 3, 2)
CHUNK = 512
BUFFERS = 4
prio_power = 0.7
weight_power = 0.5
ridge_shift = 0.5
f32, bf16 = jnp.float32, jnp.bfloat16
IN_VMEM = pl.BlockSpec(memory_space=pltpu.VMEM)
IN_SMEM = pl.BlockSpec(memory_space=pltpu.SMEM)
IN_HBM = pl.BlockSpec(memory_space=pltpu.HBM)
ROWS_BY_ROWS = (((1,), (1,)), ((), ()))


def split(value):
    high = value.astype(bf16)
    return high, (value - high.astype(f32)).astype(bf16)


def exact(left, right):
    return jnp.dot(left, right, precision=lax.Precision.HIGHEST, preferred_element_type=f32)


def row_gram(left, right):
    return lax.dot_general(left, right, ROWS_BY_ROWS, precision=lax.Precision.HIGHEST, preferred_element_type=f32)


def solve_t(matrix, rhs_block):
    block = 4
    matrix = 0.5 * (matrix + matrix.T)
    table = jnp.concatenate([matrix, rhs_block], axis=1)
    row_id = lax.broadcasted_iota(jnp.int32, table.shape, 0)
    for k in range(0, K, block):
        columns = [jnp.broadcast_to(table[:, k + j : k + j + 1], table.shape) for j in range(block)]
        rows = [table[k + i : k + i + 1, :] for i in range(block)]
        pivot = [[column[k + i : k + i + 1, :] for column in columns] for i in range(block)]
        for p in range(block):
            inverse = 1.0 / pivot[p][p]
            rows[p] = rows[p] * inverse
            pivot[p] = [value * inverse for value in pivot[p]]
            for i in range(block):
                if i != p:
                    factor = pivot[i][p]
                    rows[i] = rows[i] - factor * rows[p]
                    pivot[i] = [value - factor * over for value, over in zip(pivot[i], pivot[p])]
        for j in range(block):
            table = table - columns[j] * rows[j]
        for i in range(block):
            table = jnp.where(row_id == k + i, rows[i], table)
    return table[:, K:].T


def merged(parts):
    a, b, c, d = (part[...] for part in parts)
    return (a + b) + (c + d)


def pack(square):
    return jnp.concatenate([square[i : i + TILE] for i in range(0, K, TILE)], axis=1)


def unpack(tile):
    return jnp.concatenate([tile[:, i : i + K] for i in range(0, LANES, K)], axis=0)


def put_blocks(out, value, tile):
    blocks = value.shape[1] // LANES
    for j in range(blocks):
        out[j * K : (j + 1) * K, :] = value[:, j * LANES : (j + 1) * LANES]
    out[blocks * K :, :] = tile


def get_blocks(stacked):
    blocks = stacked.shape[0] // K
    value = jnp.concatenate([stacked[j * K : (j + 1) * K] for j in range(blocks)], axis=1)
    return value, stacked[blocks * K :]


def k1(count, ranks_hbm, targets_hbm, features, high, low, scale, out, buf, targets, ranks, pair, sem, in_sem):
    slots, width = features.shape
    steps = slots // CHUNK
    small = [
        pltpu.make_async_copy(ranks_hbm, ranks, in_sem.at[0]),
        pltpu.make_async_copy(targets_hbm, targets, in_sem.at[1]),
    ]
    copies = [
        pltpu.make_async_copy(features.at[pl.ds(c * CHUNK, CHUNK)], buf.at[c % BUFFERS], sem.at[c % BUFFERS])
        for c in range(steps)
    ]
    for copy in small:
        copy.start()
    for c in range(BUFFERS):
        copies[c].start()
    live = lax.broadcasted_iota(jnp.int32, (1, slots), 1) < count[0]
    small[0].wait()
    log_rank = jnp.log(ranks[...].astype(f32))
    scale_now = jnp.where(live, jnp.exp((prio_power * weight_power) * log_rank), 0.0)
    scale[...] = scale_now
    prio_sum = jnp.sum(jnp.where(live, jnp.exp(-prio_power * log_rank), 0.0))
    small[1].wait()
    high_t, low_t = split(targets[...] * scale_now)
    pair[0:K, :] = high_t
    pair[K : 2 * K, :] = low_t
    total = jnp.zeros((2 * K, width), f32)
    rest = jnp.zeros((K, width), f32)
    for c in range(steps):
        at = slice(c * CHUNK, (c + 1) * CHUNK)
        copies[c].wait()
        high_f, low_f = split(buf[c % BUFFERS])
        if c + BUFFERS < steps:
            copies[c + BUFFERS].start()
        high[at, :] = high_f
        low[at, :] = low_f
        total += jnp.dot(pair[:, at], high_f, preferred_element_type=f32)
        rest += jnp.dot(pair[0:K, at], low_f, preferred_element_type=f32)
    row = lax.broadcasted_iota(jnp.int32, (TILE, LANES), 0)
    col = lax.broadcasted_iota(jnp.int32, (TILE, LANES), 1)
    tail = jnp.where(col == 0, prio_sum, jnp.where(col == 1, count[0].astype(f32), 0.0))
    put_blocks(out, total[0:K] + total[K:] + rest, jnp.where(row == 0, tail, 0.0))


def put_images(field, tiles, high, low, mine, other):
    place = lax.axis_index("feat")
    x, first = place // 2, place % 2 == 0
    part = high.shape[0] // XCHIPS
    high_v, low_v = split(field)
    pair = jnp.concatenate([high_v, low_v], axis=0)
    for c in range(XCHIPS):
        slot = x ^ c
        for piece in range(0, part, CHUNK):
            at = slice(c * part + piece, c * part + piece + CHUNK)
            both = lax.dot_general(pair, high[at, :], ROWS_BY_ROWS, preferred_element_type=f32)
            rest = lax.dot_general(high_v, low[at, :], ROWS_BY_ROWS, preferred_element_type=f32)
            value = both[0:K] + both[K:] + rest
            here = jnp.where(first, value[0:HALF], value[HALF:])
            there = jnp.where(first, value[HALF:], value[0:HALF])
            for j in range(0, CHUNK, LANES):
                to = (piece + j) // LANES * HALF
                mine[slot, to : to + HALF, :] = here[:, j : j + LANES]
                other[slot, to : to + HALF, :] = there[:, j : j + LANES]
        mine[slot, part // LANES * HALF :, :] = tiles
        other[slot, part // LANES * HALF :, :] = tiles


def k2(p0, p1, p2, p3, high, low, field, norm, mine, other):
    total, tile = get_blocks(merged((p0, p1, p2, p3)))
    factor = jnp.sqrt(tile[0:1, 0:1] / tile[0:1, 1:2])
    norm[...] = jnp.broadcast_to(factor, norm.shape)
    rhs_field = total * factor
    field[...] = rhs_field
    put_images(rhs_field, pack(row_gram(rhs_field, rhs_field)), high, low, mine, other)


def get_images(near, far, part):
    first = lax.axis_index("feat") % 2 == 0
    out = []
    for j, ref in enumerate(near):
        blocks = []
        for at in range(0, part // LANES * HALF, HALF):
            a, b = ref[at : at + HALF, :], far[j, at : at + HALF, :]
            blocks.append(jnp.concatenate([jnp.where(first, a, b), jnp.where(first, b, a)], axis=0))
        out.append(jnp.concatenate(blocks, axis=1))
    return out


def back_project(images, scale, high, low, out):
    x = lax.axis_index("feat") // 2
    part, width = images[0].shape[1], high.shape[1]
    total = jnp.zeros((2 * K, width), f32)
    rest = jnp.zeros((K, width), f32)
    curve = jnp.zeros((2 * K, 2 * K), f32)
    for j, distance in enumerate(DISTANCES):
        base = pl.multiple_of((x ^ distance) * part, part)
        high_w, low_w = split(images[j] * scale[:, pl.ds(base, part)])
        high_i, low_i = split(images[j])
        pair = jnp.concatenate([high_w, low_w], axis=0)
        curve += lax.dot_general(
            pair, jnp.concatenate([high_i, low_i], axis=0), ROWS_BY_ROWS, preferred_element_type=f32
        )
        for piece in range(0, part, CHUNK):
            at = pl.ds(pl.multiple_of(base + piece, CHUNK), CHUNK)
            to = slice(piece, piece + CHUNK)
            total += jnp.dot(pair[:, to], high[at, :], preferred_element_type=f32)
            rest += jnp.dot(high_w[:, to], low[at, :], preferred_element_type=f32)
    curve = curve[0:K, 0:K] + curve[0:K, K:] + curve[K:, 0:K]
    put_blocks(out, total[0:K] + total[K:] + rest, pack(curve))


def k3(n0, n1, n2, n3, far, scale, high, low, out, kept, gram):
    part = kept.shape[2]
    gram[...] = unpack(n0[part // LANES * HALF :, :])
    images = get_images((n0, n1, n2, n3), far, part)
    for j in range(XCHIPS):
        kept[j] = images[j]
    back_project(images, scale, high, low, out)


def k4(z0, z1, z2, z3, field, norm, gram, high, low, residual, step, mine, other):
    total, tile = get_blocks(merged((z0, z1, z2, z3)))
    factor = norm[0:1, 0:1]
    curvature = unpack(tile) * factor + ridge_shift * gram[...]
    step_t = solve_t(curvature, gram[...])
    step[...] = step_t
    backward = total * factor + ridge_shift * field[...]
    now = field[...] - exact(step_t, backward)
    residual[...] = now
    tiles = jnp.concatenate([pack(row_gram(now, now)), pack(row_gram(now, field[...]))], axis=0)
    put_images(now, tiles, high, low, mine, other)


def k5(n0, n1, n2, n3, far, kept, gram, scale, high, low, out, coef, gram_new, cross):
    part = kept.shape[2]
    tiles = n0[part // LANES * HALF :, :]
    square = unpack(tiles[0:TILE])
    gram_new[...] = square
    cross[...] = unpack(tiles[TILE:])
    coef_t = solve_t(gram[...], square)
    coef[...] = coef_t
    chunks = get_images((n0, n1, n2, n3), far, part)
    images = [chunk + exact(coef_t, kept[j]) for j, chunk in enumerate(chunks)]
    back_project(images, scale, high, low, out)


def k6(z0, z1, z2, z3, field, residual, norm, gram, gram_new, cross, step, coef, solution_out, residual_out):
    coef_t = coef[...]
    mixed = row_gram(cross[...], coef_t)
    square = gram_new[...] + mixed + mixed.T + row_gram(exact(coef_t, gram[...]), coef_t)
    total, tile = get_blocks(merged((z0, z1, z2, z3)))
    factor = norm[0:1, 0:1]
    curvature = unpack(tile) * factor + ridge_shift * square
    step_t = solve_t(curvature, gram_new[...])
    direction = residual[...] + exact(coef_t, field[...])
    backward = total * factor + ridge_shift * direction
    solution_out[...] = exact(step[...], field[...]) + exact(step_t, direction)
    residual_out[...] = residual[...] - exact(step_t, backward)


def call(kernel, outs, operands, specs=None, scratch=(), limit=24):
    return pl.pallas_call(
        kernel,
        out_shape=outs,
        in_specs=specs or [IN_VMEM] * len(operands),
        out_specs=[IN_VMEM] * len(outs),
        scratch_shapes=scratch,
        compiler_params=pltpu.CompilerParams(vmem_limit_bytes=limit << 20),
        name=kernel.__name__,
    )(*operands)


def in_hbm(value):
    return pltpu.with_memory_space_constraint(value, pltpu.HBM)


def exchange(value, row_distance, feat_distance):
    pairs = [
        (r * 8 + f, (r ^ row_distance[f % 2]) * 8 + (f ^ feat_distance)) for r in range(16) for f in range(8)
    ]
    return lax.ppermute(value, ("rows", "feat"), pairs)


def gather_rows(value):
    got = {d: exchange(value, (d, 4 * d), 0) for d in (1, 3, 2)}
    value = (value + got[1]) + (got[3] + got[2])
    got = {d: exchange(value, (4 * d, d), 0) for d in (1, 3, 2)}
    return [value, got[1], got[3], got[2]]


def sum_feat(mine, other):
    here = (0, 0)
    value = mine + exchange(other, here, 1)
    got = {d: exchange(value[d], here, 2 * d) for d in (1, 3, 2)}
    value = (value[0] + got[1]) + (got[3] + got[2])
    got = {d: exchange(value, here, 2 * d) for d in (1, 3, 2)}
    near = [value, *(got[d] for d in DISTANCES[1:])]
    return [*near, exchange(jnp.stack(near), here, 1)]


def local(features, targets, counts, ranks):
    slots, width = features.shape
    part = slots // XCHIPS
    shape = jax.ShapeDtypeStruct
    summed = shape((width // LANES * K + TILE, LANES), f32)
    field_like, small = shape((K, width), f32), shape((K, K), f32)

    def images_like(tiles):
        return [shape((XCHIPS, part // LANES * HALF + tiles * TILE, LANES), f32)] * 2

    high, low, scale, out = call(
        k1,
        [pltpu.VMEM((slots, width), bf16), pltpu.VMEM((slots, width), bf16), shape((1, slots), f32), summed],
        (counts, in_hbm(ranks.reshape(1, slots)), in_hbm(targets), in_hbm(features)),
        [IN_SMEM, IN_HBM, IN_HBM, IN_HBM],
        (
            pltpu.VMEM((BUFFERS, CHUNK, width), f32),
            pltpu.VMEM((K, slots), f32),
            pltpu.VMEM((1, slots), jnp.int32),
            pltpu.VMEM((2 * K, slots), bf16),
            pltpu.SemaphoreType.DMA((BUFFERS,)),
            pltpu.SemaphoreType.DMA((2,)),
        ),
    )
    parts = gather_rows(out)
    field, norm, mine, other = call(k2, [field_like, shape((8, 128), f32), *images_like(1)], (*parts, high, low))
    parts = sum_feat(mine, other)
    out, kept, gram = call(k3, [summed, shape((XCHIPS, K, part), f32), small], (*parts, scale, high, low))
    parts = gather_rows(out)
    residual, step, mine, other = call(
        k4, [field_like, small, *images_like(2)], (*parts, field, norm, gram, high, low)
    )
    parts = sum_feat(mine, other)
    out, coef, gram_new, cross = call(
        k5, [summed, small, small, small], (*parts, kept, gram, scale, high, low)
    )
    parts = gather_rows(out)
    rest = (field, residual, norm, gram, gram_new, cross, step, coef)
    return tuple(call(k6, [field_like, field_like], (*parts, *rest)))


def solution(mesh):
    placed = (P("rows", "feat"), P(None, "rows"), P("rows"), P("rows"))
    return jax.shard_map(
        local,
        mesh=mesh,
        in_specs=placed,
        out_specs=(P(None, "feat"), P(None, "feat")),
        check_vma=False,
    )
```

```python
import jax
import jax.numpy as jnp
from jax import lax
from jax.experimental import pallas as pl
from jax.experimental.pallas import tpu as pltpu
from jax.sharding import PartitionSpec as P


K = 32
HALF = K // 2
LANES = 128
TILE = 8
XCHIPS = 4
ORDER = (2, 3, 1, 0)
FIRST = ORDER[0]
HERE = (0, 0)
CHUNK = 512
BUFFERS = 4
prio_power = 0.7
weight_power = 0.5
ridge_shift = 0.5
f32, bf16 = jnp.float32, jnp.bfloat16
IN_VMEM = pl.BlockSpec(memory_space=pltpu.VMEM)
IN_SMEM = pl.BlockSpec(memory_space=pltpu.SMEM)
IN_HBM = pl.BlockSpec(memory_space=pltpu.HBM)
ROWS_BY_ROWS = (((1,), (1,)), ((), ()))


def split(value):
    high = value.astype(bf16)
    return high, (value - high.astype(f32)).astype(bf16)


def exact(left, right):
    return jnp.dot(left, right, precision=lax.Precision.HIGHEST, preferred_element_type=f32)


def row_gram(left, right):
    return lax.dot_general(left, right, ROWS_BY_ROWS, precision=lax.Precision.HIGHEST, preferred_element_type=f32)


def solve_t(matrix, rhs_block):
    block = 4
    matrix = 0.5 * (matrix + matrix.T)
    table = jnp.concatenate([matrix, rhs_block], axis=1)
    row_id = lax.broadcasted_iota(jnp.int32, table.shape, 0)
    for k in range(0, K, block):
        columns = [jnp.broadcast_to(table[:, k + j : k + j + 1], table.shape) for j in range(block)]
        rows = [table[k + i : k + i + 1, :] for i in range(block)]
        pivot = [[column[k + i : k + i + 1, :] for column in columns] for i in range(block)]
        for p in range(block):
            inverse = 1.0 / pivot[p][p]
            rows[p] = rows[p] * inverse
            pivot[p] = [value * inverse for value in pivot[p]]
            for i in range(block):
                if i != p:
                    factor = pivot[i][p]
                    rows[i] = rows[i] - factor * rows[p]
                    pivot[i] = [value - factor * over for value, over in zip(pivot[i], pivot[p])]
        for j in range(block):
            table = table - columns[j] * rows[j]
        for i in range(block):
            table = jnp.where(row_id == k + i, rows[i], table)
    return table[:, K:].T


def merged(parts):
    a, b, c, d = (part[...] for part in parts)
    return (a + b) + (c + d)


def pack(square):
    return jnp.concatenate([square[i : i + TILE] for i in range(0, K, TILE)], axis=1)


def unpack(tile):
    return jnp.concatenate([tile[:, i : i + K] for i in range(0, LANES, K)], axis=0)


def put_blocks(out, value, tile):
    blocks = value.shape[1] // LANES
    for j in range(blocks):
        out[j * K : (j + 1) * K, :] = value[:, j * LANES : (j + 1) * LANES]
    out[blocks * K :, :] = tile


def get_blocks(stacked):
    blocks = stacked.shape[0] // K
    value = jnp.concatenate([stacked[j * K : (j + 1) * K] for j in range(blocks)], axis=1)
    return value, stacked[blocks * K :]


def k1(count, ranks_hbm, targets_hbm, features, high, low, scale, out, buf, targets, ranks, pair, sem, in_sem):
    slots, width = features.shape
    steps = slots // CHUNK
    small = [
        pltpu.make_async_copy(ranks_hbm, ranks, in_sem.at[0]),
        pltpu.make_async_copy(targets_hbm, targets, in_sem.at[1]),
    ]
    copies = [
        pltpu.make_async_copy(features.at[pl.ds(c * CHUNK, CHUNK)], buf.at[c % BUFFERS], sem.at[c % BUFFERS])
        for c in range(steps)
    ]
    for copy in small:
        copy.start()
    for c in range(BUFFERS):
        copies[c].start()
    live = lax.broadcasted_iota(jnp.int32, (1, slots), 1) < count[0]
    small[0].wait()
    log_rank = jnp.log(ranks[...].astype(f32))
    scale_now = jnp.where(live, jnp.exp((prio_power * weight_power) * log_rank), 0.0)
    scale[...] = scale_now
    prio_sum = jnp.sum(jnp.where(live, jnp.exp(-prio_power * log_rank), 0.0))
    small[1].wait()
    high_t, low_t = split(targets[...] * scale_now)
    pair[0:K, :] = high_t
    pair[K : 2 * K, :] = low_t
    total = jnp.zeros((2 * K, width), f32)
    rest = jnp.zeros((K, width), f32)
    for c in range(steps):
        at = slice(c * CHUNK, (c + 1) * CHUNK)
        copies[c].wait()
        high_f, low_f = split(buf[c % BUFFERS])
        if c + BUFFERS < steps:
            copies[c + BUFFERS].start()
        high[at, :] = high_f
        low[at, :] = low_f
        total += jnp.dot(pair[:, at], high_f, preferred_element_type=f32)
        rest += jnp.dot(pair[0:K, at], low_f, preferred_element_type=f32)
    row = lax.broadcasted_iota(jnp.int32, (TILE, LANES), 0)
    col = lax.broadcasted_iota(jnp.int32, (TILE, LANES), 1)
    tail = jnp.where(col == 0, prio_sum, jnp.where(col == 1, count[0].astype(f32), 0.0))
    put_blocks(out, total[0:K] + total[K:] + rest, jnp.where(row == 0, tail, 0.0))


def put_images(distance, pair, tiles, high, low, mine, other):
    place = lax.axis_index("feat")
    x, first = place // 2, place % 2 == 0
    part = high.shape[0] // XCHIPS
    base = pl.multiple_of((x ^ distance) * part, part)
    for piece in range(0, part, CHUNK):
        at = pl.ds(pl.multiple_of(base + piece, CHUNK), CHUNK)
        both = lax.dot_general(pair, high[at, :], ROWS_BY_ROWS, preferred_element_type=f32)
        rest = lax.dot_general(pair[0:K], low[at, :], ROWS_BY_ROWS, preferred_element_type=f32)
        value = both[0:K] + both[K:] + rest
        here = jnp.where(first, value[0:HALF], value[HALF:])
        there = jnp.where(first, value[HALF:], value[0:HALF])
        for j in range(0, CHUNK, LANES):
            to = (piece + j) // LANES * HALF
            mine[to : to + HALF, :] = here[:, j : j + LANES]
            other[to : to + HALF, :] = there[:, j : j + LANES]
    mine[part // LANES * HALF :, :] = tiles
    other[part // LANES * HALF :, :] = tiles


def put_pair(value, pair):
    high_v, low_v = split(value)
    pair[0:K, :] = high_v
    pair[K:, :] = low_v


def k2(p0, p1, p2, p3, high, low, field, norm, pair, tiles, mine, other):
    total, tile = get_blocks(merged((p0, p1, p2, p3)))
    factor = jnp.sqrt(tile[0:1, 0:1] / tile[0:1, 1:2])
    norm[...] = jnp.broadcast_to(factor, norm.shape)
    rhs_field = total * factor
    field[...] = rhs_field
    put_pair(rhs_field, pair)
    tiles[...] = pack(row_gram(rhs_field, rhs_field))
    put_images(FIRST, pair[...], tiles[...], high, low, mine, other)


def images_at(distance):
    def images_kernel(pair, tiles, high, low, mine, other):
        put_images(distance, pair[...], tiles[...], high, low, mine, other)

    return images_kernel


def get_images(near, far):
    first = lax.axis_index("feat") % 2 == 0
    blocks = []
    for at in range(0, near.shape[0], HALF):
        a, b = near[at : at + HALF, :], far[at : at + HALF, :]
        blocks.append(jnp.concatenate([jnp.where(first, a, b), jnp.where(first, b, a)], axis=0))
    return jnp.concatenate(blocks, axis=1)


def back_project(distance, images, scale, high, low, before, out):
    x = lax.axis_index("feat") // 2
    part, width = images.shape[1], high.shape[1]
    total = jnp.zeros((2 * K, width), f32)
    rest = jnp.zeros((K, width), f32)
    base = pl.multiple_of((x ^ distance) * part, part)
    high_w, low_w = split(images * scale[:, pl.ds(base, part)])
    pair = jnp.concatenate([high_w, low_w], axis=0)
    curve = lax.dot_general(pair, jnp.concatenate(split(images), axis=0), ROWS_BY_ROWS, preferred_element_type=f32)
    for piece in range(0, part, CHUNK):
        at = pl.ds(pl.multiple_of(base + piece, CHUNK), CHUNK)
        to = slice(piece, piece + CHUNK)
        total += jnp.dot(pair[:, to], high[at, :], preferred_element_type=f32)
        rest += jnp.dot(high_w[:, to], low[at, :], preferred_element_type=f32)
    value = total[0:K] + total[K:] + rest
    tile = pack(curve[0:K, 0:K] + curve[0:K, K:] + curve[K:, 0:K])
    if before is not None:
        value_before, tile_before = get_blocks(before[...])
        value, tile = value_before + value, tile_before + tile
    put_blocks(out, value, tile)


def back_at(distance, begins):
    def back_kernel(near, far, scale, high, low, *rest):
        before, (out, kept) = (None, rest) if begins else (rest[0], rest[1:])
        images = get_images(near, far)
        kept[...] = images
        back_project(distance, images, scale, high, low, before, out)

    return back_kernel


def mixed_back_at(distance, begins):
    def mixed_back_kernel(near, far, scale, high, low, coef, kept, *rest):
        before, (out,) = (None, rest) if begins else (rest[0], rest[1:])
        images = get_images(near, far) + exact(coef[...], kept[...])
        back_project(distance, images, scale, high, low, before, out)

    return mixed_back_kernel


def k4(z0, z1, z2, z3, field, norm, tile_b, high, low, residual, step, pair, tiles, mine, other):
    total, tile = get_blocks(merged((z0, z1, z2, z3)))
    factor = norm[0:1, 0:1]
    gram = unpack(tile_b[...])
    curvature = unpack(tile) * factor + ridge_shift * gram
    step_t = solve_t(curvature, gram)
    step[...] = step_t
    backward = total * factor + ridge_shift * field[...]
    now = field[...] - exact(step_t, backward)
    residual[...] = now
    put_pair(now, pair)
    tiles[0:TILE, :] = pack(row_gram(now, now))
    tiles[TILE:, :] = pack(row_gram(now, field[...]))
    put_images(FIRST, pair[...], tiles[...], high, low, mine, other)


def solve_coef(tile_b, tiles, coef):
    coef[...] = solve_t(unpack(tile_b[...]), unpack(tiles[0:TILE, :]))


def k6(z0, z1, z2, z3, field, residual, norm, tile_b, tiles, step, coef, solution_out, residual_out):
    coef_t = coef[...]
    gram_new = unpack(tiles[0:TILE, :])
    mixed = row_gram(unpack(tiles[TILE:, :]), coef_t)
    square = gram_new + mixed + mixed.T + row_gram(exact(coef_t, unpack(tile_b[...])), coef_t)
    total, tile = get_blocks(merged((z0, z1, z2, z3)))
    factor = norm[0:1, 0:1]
    curvature = unpack(tile) * factor + ridge_shift * square
    step_t = solve_t(curvature, gram_new)
    direction = residual[...] + exact(coef_t, field[...])
    backward = total * factor + ridge_shift * direction
    solution_out[...] = exact(step[...], field[...]) + exact(step_t, direction)
    residual_out[...] = residual[...] - exact(step_t, backward)


def call(kernel, outs, operands, specs=None, scratch=(), passes=0.0):
    cost = pl.CostEstimate(
        flops=int(passes * 3 * 2 * K * 4096 * 1024), bytes_accessed=int(passes * (1 << 24)), transcendentals=0
    )
    return pl.pallas_call(
        kernel,
        out_shape=outs,
        in_specs=specs or [IN_VMEM] * len(operands),
        out_specs=[IN_VMEM] * len(outs),
        scratch_shapes=scratch,
        compiler_params=pltpu.CompilerParams(vmem_limit_bytes=24 << 20),
        cost_estimate=cost,
        name=kernel.__name__,
    )(*operands)


def in_hbm(value):
    return pltpu.with_memory_space_constraint(value, pltpu.HBM)


def exchange(value, row_distance, feat_distance):
    pairs = [
        (r * 8 + f, (r ^ row_distance[f % 2]) * 8 + (f ^ feat_distance)) for r in range(16) for f in range(8)
    ]
    return lax.ppermute(value, ("rows", "feat"), pairs)


def gather_rows(value):
    got = {d: exchange(value, (d, 4 * d), 0) for d in (1, 3, 2)}
    value = (value + got[1]) + (got[3] + got[2])
    got = {d: exchange(value, (4 * d, d), 0) for d in (1, 3, 2)}
    return [value, got[1], got[3], got[2]]


def after(value, *earlier):
    return lax.optimization_barrier((value, *earlier))[0]


def sum_feat(first, images, pair, body):
    got, sent, waits = {}, {}, ()
    for distance in ORDER:
        mine, other = first if distance == FIRST else images(distance, after(pair, *waits))
        other = exchange(other, HERE, 1)
        if distance:
            sent[distance] = mine + other
            got[distance] = exchange(sent[distance], HERE, 2 * distance)
        waits = {ORDER[1]: (sent[FIRST],), ORDER[2]: tuple(sent.values())}.get(distance, ())
    tiles = (sent[FIRST][body:] + got[1][body:]) + (got[3][body:] + got[2][body:])
    return ((mine[0:body] + got[1][0:body]) + (got[3][0:body] + got[2][0:body])) + other[0:body], tiles


def spread_feat(value, project):
    got = {d: exchange(value, HERE, 2 * d) if d else value for d in ORDER}
    before = ()
    far = {d: exchange(got[d], HERE, 1) for d in (0, 1)}
    for d, then in ((0, 3), (1, 2), (3, None), (2, None)):
        before = project(d, got[d], far[d], before)
        if then is not None:
            far[then] = exchange(after(got[then], *before), HERE, 1)
    return before


def local(features, targets, counts, ranks):
    slots, width = features.shape
    part = slots // XCHIPS
    body = part // LANES * HALF
    shape = jax.ShapeDtypeStruct
    summed = shape((width // LANES * K + TILE, LANES), f32)
    field_like, small = shape((K, width), f32), shape((K, K), f32)
    pair_like = shape((2 * K, width), bf16)
    share = 1.0 / XCHIPS

    def tiles_like(tiles):
        return shape((tiles * TILE, LANES), f32)

    def images_like(tiles):
        return [shape((body + tiles * TILE, LANES), f32)] * 2

    high, low, scale, out = call(
        k1,
        [pltpu.VMEM((slots, width), bf16), pltpu.VMEM((slots, width), bf16), shape((1, slots), f32), summed],
        (counts, in_hbm(ranks.reshape(1, slots)), in_hbm(targets), in_hbm(features)),
        [IN_SMEM, IN_HBM, IN_HBM, IN_HBM],
        (
            pltpu.VMEM((BUFFERS, CHUNK, width), f32),
            pltpu.VMEM((K, slots), f32),
            pltpu.VMEM((1, slots), jnp.int32),
            pltpu.VMEM((2 * K, slots), bf16),
            pltpu.SemaphoreType.DMA((BUFFERS,)),
            pltpu.SemaphoreType.DMA((2,)),
        ),
        1.0,
    )

    def images(tiles):
        def of(distance, pair):
            count = tiles.shape[0] // TILE
            return call(images_at(distance), images_like(count), (pair, tiles, high, low), passes=share)

        return of

    parts = gather_rows(out)
    field, norm, pair, tiles, *first = call(
        k2,
        [field_like, tiles_like(1), pair_like, tiles_like(1), *images_like(1)],
        (*parts, high, low),
        passes=share,
    )
    own, tile_b = sum_feat(first, images(tiles), pair, body)
    kept = {}

    def project(distance, near, far, before):
        out, kept[distance] = call(
            back_at(distance, not before),
            [summed, shape((K, part), f32)],
            (near, far, scale, high, low, *before),
            passes=share,
        )
        return (out,)

    parts = gather_rows(*spread_feat(own, project))
    residual, step, pair, tiles, *first = call(
        k4,
        [field_like, small, pair_like, tiles_like(2), *images_like(2)],
        (*parts, field, norm, tile_b, high, low),
        passes=share,
    )
    own, tiles = sum_feat(first, images(tiles), pair, body)
    (coef,) = call(solve_coef, [small], (tile_b, tiles), passes=share)

    def mixed_project(distance, near, far, before):
        return call(
            mixed_back_at(distance, not before),
            [summed],
            (near, far, scale, high, low, coef, kept[distance], *before),
            passes=share,
        )

    parts = gather_rows(*spread_feat(own, mixed_project))
    rest = (field, residual, norm, tile_b, tiles, step, coef)
    return tuple(call(k6, [field_like, field_like], (*parts, *rest)))


def solution(mesh):
    placed = (P("rows", "feat"), P(None, "rows"), P("rows"), P("rows"))
    return jax.shard_map(
        local,
        mesh=mesh,
        in_specs=placed,
        out_specs=(P(None, "feat"), P(None, "feat")),
        check_vma=False,
    )
```

```python
import jax
import jax.numpy as jnp
from jax import lax
from jax.experimental import pallas as pl
from jax.experimental.pallas import tpu as pltpu
from jax.sharding import PartitionSpec as P


K = 32
HALF = K // 2
LANES = 128
TILE = 8
XCHIPS = 4
ORDER = (2, 3, 1, 0)
FIRST = ORDER[0]
HERE = (0, 0)
CHUNK = 512
STREAM = 256
BUFFERS = 8
prio_power = 0.7
weight_power = 0.5
ridge_shift = 0.5
f32, bf16 = jnp.float32, jnp.bfloat16
IN_VMEM = pl.BlockSpec(memory_space=pltpu.VMEM)
IN_SMEM = pl.BlockSpec(memory_space=pltpu.SMEM)
IN_HBM = pl.BlockSpec(memory_space=pltpu.HBM)
ROWS_BY_ROWS = (((1,), (1,)), ((), ()))


def split(value):
    high = value.astype(bf16)
    return high, (value - high.astype(f32)).astype(bf16)


def exact(left, right):
    return jnp.dot(left, right, precision=lax.Precision.HIGHEST, preferred_element_type=f32)


def row_gram(left, right):
    return lax.dot_general(left, right, ROWS_BY_ROWS, precision=lax.Precision.HIGHEST, preferred_element_type=f32)


def solve_t(matrix, rhs_block):
    matrix = 0.5 * (matrix + matrix.T)
    table = jnp.concatenate([matrix, rhs_block], axis=1)
    for k in range(0, K, TILE):
        columns = [jnp.broadcast_to(table[:, k + j : k + j + 1], table.shape) for j in range(TILE)]
        rows = [table[k + i : k + i + 1, :] for i in range(TILE)]
        pivot = [[column[k + i : k + i + 1, :] for column in columns] for i in range(TILE)]
        for p in range(TILE):
            inverse = 1.0 / pivot[p][p]
            rows[p] = rows[p] * inverse
            pivot[p] = [value * inverse for value in pivot[p]]
            for i in range(TILE):
                if i != p:
                    factor = pivot[i][p]
                    rows[i] = rows[i] - factor * rows[p]
                    for j in range(p + 1, TILE):
                        pivot[i][j] = pivot[i][j] - factor * pivot[p][j]
        change = columns[0] * rows[0]
        for j in range(1, TILE):
            change = change + columns[j] * rows[j]
        table = table - change
        pieces = [table[0:k], *rows, table[k + TILE :]]
        table = jnp.concatenate([piece for piece in pieces if piece.shape[0]], axis=0)
    return table[:, K:].T


def merged(parts):
    a, b, c, d = (part[...] for part in parts)
    return (a + b) + (c + d)


def pack(square):
    return jnp.concatenate([square[i : i + TILE] for i in range(0, K, TILE)], axis=1)


def unpack(tile):
    return jnp.concatenate([tile[:, i : i + K] for i in range(0, LANES, K)], axis=0)


def put_blocks(out, value, tile):
    blocks = value.shape[1] // LANES
    for j in range(blocks):
        out[j * K : (j + 1) * K, :] = value[:, j * LANES : (j + 1) * LANES]
    out[blocks * K :, :] = tile


def get_blocks(stacked):
    blocks = stacked.shape[0] // K
    value = jnp.concatenate([stacked[j * K : (j + 1) * K] for j in range(blocks)], axis=1)
    return value, stacked[blocks * K :]


def k1(count, ranks_hbm, targets_hbm, features, high, low, scale, out, buf, targets, ranks, sem, in_sem):
    slots, width = features.shape
    steps = slots // STREAM
    small = [
        pltpu.make_async_copy(ranks_hbm, ranks, in_sem.at[0]),
        pltpu.make_async_copy(targets_hbm, targets, in_sem.at[1]),
    ]
    copies = [
        pltpu.make_async_copy(features.at[pl.ds(c * STREAM, STREAM)], buf.at[c % BUFFERS], sem.at[c % BUFFERS])
        for c in range(steps)
    ]
    for copy in small:
        copy.start()
    for c in range(BUFFERS):
        copies[c].start()
    live = lax.broadcasted_iota(jnp.int32, (1, slots), 1) < count[0]
    small[0].wait()
    log_rank = jnp.log(ranks[...].astype(f32))
    scale_now = jnp.where(live, jnp.exp((prio_power * weight_power) * log_rank), 0.0)
    scale[...] = scale_now
    prio_sum = jnp.sum(jnp.where(live, jnp.exp(-prio_power * log_rank), 0.0))
    small[1].wait()
    total = jnp.zeros((2 * K, width), f32)
    rest = jnp.zeros((K, width), f32)
    for c in range(steps):
        at = slice(c * STREAM, (c + 1) * STREAM)
        high_t, low_t = split(targets[:, at] * scale_now[:, at])
        copies[c].wait()
        high_f, low_f = split(buf[c % BUFFERS])
        if c + BUFFERS < steps:
            copies[c + BUFFERS].start()
        high[at, :] = high_f
        low[at, :] = low_f
        total += jnp.dot(jnp.concatenate([high_t, low_t], axis=0), high_f, preferred_element_type=f32)
        rest += jnp.dot(high_t, low_f, preferred_element_type=f32)
    row = lax.broadcasted_iota(jnp.int32, (TILE, LANES), 0)
    col = lax.broadcasted_iota(jnp.int32, (TILE, LANES), 1)
    tail = jnp.where(col == 0, prio_sum, jnp.where(col == 1, count[0].astype(f32), 0.0))
    put_blocks(out, total[0:K] + total[K:] + rest, jnp.where(row == 0, tail, 0.0))


def put_images(distance, pair, tiles, high, low, mine, other):
    place = lax.axis_index("feat")
    x, first = place // 2, place % 2 == 0
    part = high.shape[0] // XCHIPS
    base = pl.multiple_of((x ^ distance) * part, part)
    for piece in range(0, part, CHUNK):
        at = pl.ds(pl.multiple_of(base + piece, CHUNK), CHUNK)
        both = lax.dot_general(pair, high[at, :], ROWS_BY_ROWS, preferred_element_type=f32)
        rest = lax.dot_general(pair[0:K], low[at, :], ROWS_BY_ROWS, preferred_element_type=f32)
        value = both[0:K] + both[K:] + rest
        here = jnp.where(first, value[0:HALF], value[HALF:])
        there = jnp.where(first, value[HALF:], value[0:HALF])
        for j in range(0, CHUNK, LANES):
            to = (piece + j) // LANES * HALF
            mine[to : to + HALF, :] = here[:, j : j + LANES]
            other[to : to + HALF, :] = there[:, j : j + LANES]
    mine[part // LANES * HALF :, :] = tiles
    other[part // LANES * HALF :, :] = tiles


def put_pair(value, pair):
    high_v, low_v = split(value)
    pair[0:K, :] = high_v
    pair[K:, :] = low_v


def k2(p0, p1, p2, p3, high, low, field, norm, pair, tiles, mine, other):
    total, tile = get_blocks(merged((p0, p1, p2, p3)))
    factor = jnp.sqrt(tile[0:1, 0:1] / tile[0:1, 1:2])
    norm[...] = jnp.broadcast_to(factor, norm.shape)
    rhs_field = total * factor
    field[...] = rhs_field
    put_pair(rhs_field, pair)
    tiles[...] = pack(row_gram(rhs_field, rhs_field))
    put_images(FIRST, pair[...], tiles[...], high, low, mine, other)


def images_at(distance):
    def images_kernel(pair, tiles, high, low, mine, other):
        put_images(distance, pair[...], tiles[...], high, low, mine, other)

    return images_kernel


def get_images(near, far):
    first = lax.axis_index("feat") % 2 == 0
    blocks = []
    for at in range(0, near.shape[0], HALF):
        a, b = near[at : at + HALF, :], far[at : at + HALF, :]
        blocks.append(jnp.concatenate([jnp.where(first, a, b), jnp.where(first, b, a)], axis=0))
    return jnp.concatenate(blocks, axis=1)


def back_project(distance, images, scale, high, low, before, out):
    x = lax.axis_index("feat") // 2
    part, width = images.shape[1], high.shape[1]
    total = jnp.zeros((2 * K, width), f32)
    rest = jnp.zeros((K, width), f32)
    base = pl.multiple_of((x ^ distance) * part, part)
    high_w, low_w = split(images * scale[:, pl.ds(base, part)])
    pair = jnp.concatenate([high_w, low_w], axis=0)
    curve = lax.dot_general(pair, jnp.concatenate(split(images), axis=0), ROWS_BY_ROWS, preferred_element_type=f32)
    for piece in range(0, part, CHUNK):
        at = pl.ds(pl.multiple_of(base + piece, CHUNK), CHUNK)
        to = slice(piece, piece + CHUNK)
        total += jnp.dot(pair[:, to], high[at, :], preferred_element_type=f32)
        rest += jnp.dot(high_w[:, to], low[at, :], preferred_element_type=f32)
    value = total[0:K] + total[K:] + rest
    tile = pack(curve[0:K, 0:K] + curve[0:K, K:] + curve[K:, 0:K])
    if before is not None:
        value_before, tile_before = get_blocks(before[...])
        value, tile = value_before + value, tile_before + tile
    put_blocks(out, value, tile)


def back_at(distance, begins):
    def back_kernel(near, far, scale, high, low, *rest):
        before, (out, kept) = (None, rest) if begins else (rest[0], rest[1:])
        images = get_images(near, far)
        kept[...] = images
        back_project(distance, images, scale, high, low, before, out)

    return back_kernel


def mixed_back_at(distance, begins):
    def mixed_back_kernel(near, far, scale, high, low, coef, kept, *rest):
        before, (out,) = (None, rest) if begins else (rest[0], rest[1:])
        images = get_images(near, far) + exact(coef[...], kept[...])
        back_project(distance, images, scale, high, low, before, out)

    return mixed_back_kernel


def k4(z0, z1, z2, z3, field, norm, tile_b, high, low, residual, step, pair, tiles, mine, other):
    total, tile = get_blocks(merged((z0, z1, z2, z3)))
    factor = norm[0:1, 0:1]
    gram = unpack(tile_b[...])
    curvature = unpack(tile) * factor + ridge_shift * gram
    step_t = solve_t(curvature, gram)
    step[...] = step_t
    backward = total * factor + ridge_shift * field[...]
    now = field[...] - exact(step_t, backward)
    residual[...] = now
    put_pair(now, pair)
    tiles[0:TILE, :] = pack(row_gram(now, now))
    tiles[TILE:, :] = pack(row_gram(now, field[...]))
    put_images(FIRST, pair[...], tiles[...], high, low, mine, other)


def solve_coef(tile_b, tiles, coef):
    coef[...] = solve_t(unpack(tile_b[...]), unpack(tiles[0:TILE, :]))


def prepare(field, residual, tile_b, tiles, step, coef, begun, direction, square):
    coef_t = coef[...]
    mixed = row_gram(unpack(tiles[TILE:, :]), coef_t)
    square[...] = unpack(tiles[0:TILE, :]) + mixed + mixed.T + row_gram(exact(coef_t, unpack(tile_b[...])), coef_t)
    direction[...] = residual[...] + exact(coef_t, field[...])
    begun[...] = exact(step[...], field[...])


def k6(z0, z1, z2, z3, residual, norm, tiles, begun, direction, square, solution_out, residual_out):
    total, tile = get_blocks(merged((z0, z1, z2, z3)))
    factor = norm[0:1, 0:1]
    curvature = unpack(tile) * factor + ridge_shift * square[...]
    step_t = solve_t(curvature, unpack(tiles[0:TILE, :]))
    backward = total * factor + ridge_shift * direction[...]
    solution_out[...] = begun[...] + exact(step_t, direction[...])
    residual_out[...] = residual[...] - exact(step_t, backward)


def call(kernel, outs, operands, specs=None, scratch=(), passes=0.0):
    cost = pl.CostEstimate(
        flops=int(passes * 3 * 2 * K * 4096 * 1024), bytes_accessed=int(passes * (1 << 24)), transcendentals=0
    )
    return pl.pallas_call(
        kernel,
        out_shape=outs,
        in_specs=specs or [IN_VMEM] * len(operands),
        out_specs=[IN_VMEM] * len(outs),
        scratch_shapes=scratch,
        compiler_params=pltpu.CompilerParams(vmem_limit_bytes=24 << 20),
        cost_estimate=cost,
        name=kernel.__name__,
    )(*operands)


def in_hbm(value):
    return pltpu.with_memory_space_constraint(value, pltpu.HBM)


def exchange(value, row_distance, feat_distance):
    pairs = [
        (r * 8 + f, (r ^ row_distance[f % 2]) * 8 + (f ^ feat_distance)) for r in range(16) for f in range(8)
    ]
    return lax.ppermute(value, ("rows", "feat"), pairs)


def gather_rows(value):
    got = {d: exchange(value, (d, 4 * d), 0) for d in (1, 3, 2)}
    value = (value + got[1]) + (got[3] + got[2])
    got = {d: exchange(value, (4 * d, d), 0) for d in (1, 3, 2)}
    return [value, got[1], got[3], got[2]]


def after(value, *earlier):
    return lax.optimization_barrier((value, *earlier))[0]


def sum_feat(first, images, pair, body):
    got, sent, waits = {}, {}, ()
    for distance in ORDER:
        mine, other = first if distance == FIRST else images(distance, after(pair, *waits))
        other = exchange(other, HERE, 1)
        if distance:
            sent[distance] = mine + other
            got[distance] = exchange(sent[distance], HERE, 2 * distance)
        waits = {ORDER[1]: (sent[FIRST],), ORDER[2]: tuple(sent.values())}.get(distance, ())
    tiles = (sent[FIRST][body:] + got[1][body:]) + (got[3][body:] + got[2][body:])
    return ((mine[0:body] + got[1][0:body]) + (got[3][0:body] + got[2][0:body])) + other[0:body], tiles


def spread_feat(value, project):
    got = {d: exchange(value, HERE, 2 * d) if d else value for d in ORDER}
    far = {0: exchange(got[0], HERE, 1)}
    before = project(0, got[0], far[0], ())
    for d in (2, 3, 1):
        far[d] = exchange(after(got[d], *before), HERE, 1)
    for d in (2, 3, 1):
        before = project(d, got[d], far[d], before)
    return before


def local(features, targets, counts, ranks):
    slots, width = features.shape
    part = slots // XCHIPS
    body = part // LANES * HALF
    shape = jax.ShapeDtypeStruct
    summed = shape((width // LANES * K + TILE, LANES), f32)
    field_like, small = shape((K, width), f32), shape((K, K), f32)
    pair_like = shape((2 * K, width), bf16)
    share = 1.0 / XCHIPS

    def tiles_like(tiles):
        return shape((tiles * TILE, LANES), f32)

    def images_like(tiles):
        return [shape((body + tiles * TILE, LANES), f32)] * 2

    high, low, scale, out = call(
        k1,
        [pltpu.VMEM((slots, width), bf16), pltpu.VMEM((slots, width), bf16), shape((1, slots), f32), summed],
        (counts, in_hbm(ranks.reshape(1, slots)), in_hbm(targets), in_hbm(features)),
        [IN_SMEM, IN_HBM, IN_HBM, IN_HBM],
        (
            pltpu.VMEM((BUFFERS, STREAM, width), f32),
            pltpu.VMEM((K, slots), f32),
            pltpu.VMEM((1, slots), jnp.int32),
            pltpu.SemaphoreType.DMA((BUFFERS,)),
            pltpu.SemaphoreType.DMA((2,)),
        ),
        1.0,
    )

    def images(tiles):
        def of(distance, pair):
            count = tiles.shape[0] // TILE
            return call(images_at(distance), images_like(count), (pair, tiles, high, low), passes=share)

        return of

    parts = gather_rows(out)
    field, norm, pair, tiles, *first = call(
        k2,
        [field_like, tiles_like(1), pair_like, tiles_like(1), *images_like(1)],
        (*parts, high, low),
        passes=share,
    )
    own, tile_b = sum_feat(first, images(tiles), pair, body)
    kept = {}

    def project(distance, near, far, before):
        out, kept[distance] = call(
            back_at(distance, not before),
            [summed, shape((K, part), f32)],
            (near, far, scale, high, low, *before),
            passes=share if before else share,
        )
        return (out,)

    parts = gather_rows(*spread_feat(own, project))
    residual, step, pair, tiles, *first = call(
        k4,
        [field_like, small, pair_like, tiles_like(2), *images_like(2)],
        (*parts, field, norm, tile_b, high, low),
        passes=share,
    )
    own, tiles = sum_feat(first, images(tiles), pair, body)
    (coef,) = call(solve_coef, [small], (tile_b, tiles), passes=share)

    def mixed_project(distance, near, far, before):
        return call(
            mixed_back_at(distance, not before),
            [summed],
            (near, far, scale, high, low, coef, kept[distance], *before),
            passes=share,
        )

    parts = gather_rows(*spread_feat(own, mixed_project))
    ready = call(prepare, [field_like, field_like, small], (field, residual, tile_b, tiles, step, coef))
    return tuple(call(k6, [field_like, field_like], (*parts, residual, norm, tiles, *ready)))


def solution(mesh):
    placed = (P("rows", "feat"), P(None, "rows"), P("rows"), P("rows"))
    return jax.shard_map(
        local,
        mesh=mesh,
        in_specs=placed,
        out_specs=(P(None, "feat"), P(None, "feat")),
        check_vma=False,
    )
```

```python
import jax
import jax.numpy as jnp
from jax import lax
from jax.experimental import pallas as pl
from jax.experimental.pallas import tpu as pltpu
from jax.sharding import PartitionSpec as P


K = 32
HALF = K // 2
LANES = 128
TILE = 8
XCHIPS = 4
ORDER = (2, 3, 1, 0)
FIRST = ORDER[0]
HERE = (0, 0)
CHUNK = 512
STREAM = 256
BUFFERS = 8
prio_power = 0.7
weight_power = 0.5
ridge_shift = 0.5
f32, bf16 = jnp.float32, jnp.bfloat16
IN_VMEM = pl.BlockSpec(memory_space=pltpu.VMEM)
IN_SMEM = pl.BlockSpec(memory_space=pltpu.SMEM)
IN_HBM = pl.BlockSpec(memory_space=pltpu.HBM)
ROWS_BY_ROWS = (((1,), (1,)), ((), ()))


def split(value):
    high = value.astype(bf16)
    return high, (value - high.astype(f32)).astype(bf16)


def exact(left, right):
    return jnp.dot(left, right, precision=lax.Precision.HIGHEST, preferred_element_type=f32)


def row_gram(left, right):
    return lax.dot_general(left, right, ROWS_BY_ROWS, precision=lax.Precision.HIGHEST, preferred_element_type=f32)


def solve_t(matrix, rhs_block):
    matrix = 0.5 * (matrix + matrix.T)
    table = jnp.concatenate([matrix, rhs_block], axis=1)
    for k in range(0, K, TILE):
        columns = [jnp.broadcast_to(table[:, k + j : k + j + 1], table.shape) for j in range(TILE)]
        rows = [table[k + i : k + i + 1, :] for i in range(TILE)]
        pivot = [[column[k + i : k + i + 1, :] for column in columns] for i in range(TILE)]
        for p in range(TILE):
            inverse = 1.0 / pivot[p][p]
            rows[p] = rows[p] * inverse
            pivot[p] = [value * inverse for value in pivot[p]]
            for i in range(TILE):
                if i != p:
                    factor = pivot[i][p]
                    rows[i] = rows[i] - factor * rows[p]
                    for j in range(p + 1, TILE):
                        pivot[i][j] = pivot[i][j] - factor * pivot[p][j]
        change = columns[0] * rows[0]
        for j in range(1, TILE):
            change = change + columns[j] * rows[j]
        table = table - change
        pieces = [table[0:k], *rows, table[k + TILE :]]
        table = jnp.concatenate([piece for piece in pieces if piece.shape[0]], axis=0)
    return table[:, K:].T


def merged(parts):
    a, b, c, d = (part[...] for part in parts)
    return (a + b) + (c + d)


def pack(square):
    return jnp.concatenate([square[i : i + TILE] for i in range(0, K, TILE)], axis=1)


def unpack(tile):
    return jnp.concatenate([tile[:, i : i + K] for i in range(0, LANES, K)], axis=0)


def put_blocks(out, value, tile):
    blocks = value.shape[1] // LANES
    for j in range(blocks):
        out[j * K : (j + 1) * K, :] = value[:, j * LANES : (j + 1) * LANES]
    out[blocks * K :, :] = tile


def get_blocks(stacked):
    blocks = stacked.shape[0] // K
    value = jnp.concatenate([stacked[j * K : (j + 1) * K] for j in range(blocks)], axis=1)
    return value, stacked[blocks * K :]


def k1(count, ranks_hbm, targets_hbm, features, high, low, scale, out, buf, targets, ranks, sem, in_sem):
    slots, width = features.shape
    steps = slots // STREAM
    small = [
        pltpu.make_async_copy(ranks_hbm, ranks, in_sem.at[0]),
        pltpu.make_async_copy(targets_hbm, targets, in_sem.at[1]),
    ]
    copies = [
        pltpu.make_async_copy(features.at[pl.ds(c * STREAM, STREAM)], buf.at[c % BUFFERS], sem.at[c % BUFFERS])
        for c in range(steps)
    ]
    for copy in small:
        copy.start()
    for c in range(BUFFERS):
        copies[c].start()
    live = lax.broadcasted_iota(jnp.int32, (1, slots), 1) < count[0]
    small[0].wait()
    log_rank = jnp.log(ranks[...].astype(f32))
    scale_now = jnp.where(live, jnp.exp((prio_power * weight_power) * log_rank), 0.0)
    scale[...] = scale_now
    prio_sum = jnp.sum(jnp.where(live, jnp.exp(-prio_power * log_rank), 0.0))
    small[1].wait()
    total = jnp.zeros((2 * K, width), f32)
    rest = jnp.zeros((K, width), f32)
    for c in range(steps):
        at = slice(c * STREAM, (c + 1) * STREAM)
        high_t, low_t = split(targets[:, at] * scale_now[:, at])
        copies[c].wait()
        high_f, low_f = split(buf[c % BUFFERS])
        if c + BUFFERS < steps:
            copies[c + BUFFERS].start()
        high[at, :] = high_f
        low[at, :] = low_f
        total += jnp.dot(jnp.concatenate([high_t, low_t], axis=0), high_f, preferred_element_type=f32)
        rest += jnp.dot(high_t, low_f, preferred_element_type=f32)
    row = lax.broadcasted_iota(jnp.int32, (TILE, LANES), 0)
    col = lax.broadcasted_iota(jnp.int32, (TILE, LANES), 1)
    tail = jnp.where(col == 0, prio_sum, jnp.where(col == 1, count[0].astype(f32), 0.0))
    put_blocks(out, total[0:K] + total[K:] + rest, jnp.where(row == 0, tail, 0.0))


def put_images(distance, pair, tiles, high, low, mine, other):
    place = lax.axis_index("feat")
    x, first = place // 2, place % 2 == 0
    part = high.shape[0] // XCHIPS
    base = pl.multiple_of((x ^ distance) * part, part)
    for piece in range(0, part, CHUNK):
        at = pl.ds(pl.multiple_of(base + piece, CHUNK), CHUNK)
        both = lax.dot_general(pair, high[at, :], ROWS_BY_ROWS, preferred_element_type=f32)
        rest = lax.dot_general(pair[0:K], low[at, :], ROWS_BY_ROWS, preferred_element_type=f32)
        value = both[0:K] + both[K:] + rest
        here = jnp.where(first, value[0:HALF], value[HALF:])
        there = jnp.where(first, value[HALF:], value[0:HALF])
        for j in range(0, CHUNK, LANES):
            to = (piece + j) // LANES * HALF
            mine[to : to + HALF, :] = here[:, j : j + LANES]
            other[to : to + HALF, :] = there[:, j : j + LANES]
    mine[part // LANES * HALF :, :] = tiles
    other[part // LANES * HALF :, :] = tiles


def put_pair(value, pair):
    high_v, low_v = split(value)
    pair[0:K, :] = high_v
    pair[K:, :] = low_v


def k2(p0, p1, p2, p3, high, low, field, norm, pair, tiles, mine, other):
    total, tile = get_blocks(merged((p0, p1, p2, p3)))
    factor = jnp.sqrt(tile[0:1, 0:1] / tile[0:1, 1:2])
    norm[...] = jnp.broadcast_to(factor, norm.shape)
    rhs_field = total * factor
    field[...] = rhs_field
    put_pair(rhs_field, pair)
    tiles[...] = pack(row_gram(rhs_field, rhs_field))
    put_images(FIRST, pair[...], tiles[...], high, low, mine, other)


def images_at(distance):
    def images_kernel(pair, tiles, high, low, mine, other):
        put_images(distance, pair[...], tiles[...], high, low, mine, other)

    return images_kernel


def get_images(near, far):
    first = lax.axis_index("feat") % 2 == 0
    blocks = []
    for at in range(0, near.shape[0], HALF):
        a, b = near[at : at + HALF, :], far[at : at + HALF, :]
        blocks.append(jnp.concatenate([jnp.where(first, a, b), jnp.where(first, b, a)], axis=0))
    return jnp.concatenate(blocks, axis=1)


def back_project(distance, images, scale, high, low, before, out):
    x = lax.axis_index("feat") // 2
    part, width = images.shape[1], high.shape[1]
    total = jnp.zeros((2 * K, width), f32)
    rest = jnp.zeros((K, width), f32)
    base = pl.multiple_of((x ^ distance) * part, part)
    high_w, low_w = split(images * scale[:, pl.ds(base, part)])
    pair = jnp.concatenate([high_w, low_w], axis=0)
    curve = lax.dot_general(pair, jnp.concatenate(split(images), axis=0), ROWS_BY_ROWS, preferred_element_type=f32)
    for piece in range(0, part, CHUNK):
        at = pl.ds(pl.multiple_of(base + piece, CHUNK), CHUNK)
        to = slice(piece, piece + CHUNK)
        total += jnp.dot(pair[:, to], high[at, :], preferred_element_type=f32)
        rest += jnp.dot(high_w[:, to], low[at, :], preferred_element_type=f32)
    value = total[0:K] + total[K:] + rest
    tile = pack(curve[0:K, 0:K] + curve[0:K, K:] + curve[K:, 0:K])
    if before is not None:
        value_before, tile_before = get_blocks(before[...])
        value, tile = value_before + value, tile_before + tile
    put_blocks(out, value, tile)


def back_at(distance, begins):
    def back_kernel(near, far, scale, high, low, *rest):
        before, (out, kept) = (None, rest) if begins else (rest[0], rest[1:])
        images = get_images(near, far)
        kept[...] = images
        back_project(distance, images, scale, high, low, before, out)

    return back_kernel


def mixed_back_at(distance, begins):
    def mixed_back_kernel(near, far, scale, high, low, mix, kept, *rest):
        before, (out,) = (None, rest) if begins else (rest[0], rest[1:])
        was = kept[...]
        images = was + exact(mix[...], jnp.concatenate([was, get_images(near, far)], axis=0))
        back_project(distance, images, scale, high, low, before, out)

    return mixed_back_kernel


def k4(z0, z1, z2, z3, field, norm, high, low, applied, curve, pair, tiles, mine, other):
    total, tile = get_blocks(merged((z0, z1, z2, z3)))
    factor = norm[0:1, 0:1]
    curve[...] = tile * factor
    backward = total * factor + ridge_shift * field[...]
    applied[...] = backward
    put_pair(backward, pair)
    tiles[0:TILE, :] = pack(row_gram(backward, backward))
    tiles[TILE:, :] = pack(row_gram(backward, field[...]))
    put_images(FIRST, pair[...], tiles[...], high, low, mine, other)


def first_step(curve, tile_b, step):
    gram = unpack(tile_b[...])
    step[...] = solve_t(unpack(curve[...]) + ridge_shift * gram, gram)


def solve_coef(tile_b, tiles, step, mix, gram_new, cross):
    gram, step_t = unpack(tile_b[...]), step[...]
    moved = exact(step_t, unpack(tiles[TILE:, :]))
    square = gram - moved - moved.T + row_gram(exact(step_t, unpack(tiles[0:TILE, :])), step_t)
    gram_new[...] = square
    cross[...] = gram - moved
    mix[...] = jnp.concatenate([solve_t(gram, square), -step_t], axis=1)


def prepare(field, applied, tile_b, mix, gram_new, cross, step, residual, begun, direction, square):
    coef_t = mix[:, 0:K]
    mixed = row_gram(cross[...], coef_t)
    square[...] = gram_new[...] + mixed + mixed.T + row_gram(exact(coef_t, unpack(tile_b[...])), coef_t)
    now = field[...] - exact(step[...], applied[...])
    residual[...] = now
    direction[...] = now + exact(coef_t, field[...])
    begun[...] = exact(step[...], field[...])


def k6(z0, z1, z2, z3, norm, gram_new, residual, begun, direction, square, solution_out, residual_out):
    total, tile = get_blocks(merged((z0, z1, z2, z3)))
    factor = norm[0:1, 0:1]
    curvature = unpack(tile) * factor + ridge_shift * square[...]
    step_t = solve_t(curvature, gram_new[...])
    backward = total * factor + ridge_shift * direction[...]
    solution_out[...] = begun[...] + exact(step_t, direction[...])
    residual_out[...] = residual[...] - exact(step_t, backward)


def call(kernel, outs, operands, specs=None, scratch=(), passes=0.0):
    cost = pl.CostEstimate(
        flops=int(passes * 3 * 2 * K * 4096 * 1024), bytes_accessed=int(passes * (1 << 24)), transcendentals=0
    )
    return pl.pallas_call(
        kernel,
        out_shape=outs,
        in_specs=specs or [IN_VMEM] * len(operands),
        out_specs=[IN_VMEM] * len(outs),
        scratch_shapes=scratch,
        compiler_params=pltpu.CompilerParams(vmem_limit_bytes=24 << 20),
        cost_estimate=cost,
        name=kernel.__name__,
    )(*operands)


def in_hbm(value):
    return pltpu.with_memory_space_constraint(value, pltpu.HBM)


def exchange(value, row_distance, feat_distance):
    pairs = [
        (r * 8 + f, (r ^ row_distance[f % 2]) * 8 + (f ^ feat_distance)) for r in range(16) for f in range(8)
    ]
    return lax.ppermute(value, ("rows", "feat"), pairs)


def gather_rows(value):
    got = {d: exchange(value, (d, 4 * d), 0) for d in (1, 3, 2)}
    value = (value + got[1]) + (got[3] + got[2])
    got = {d: exchange(value, (4 * d, d), 0) for d in (1, 3, 2)}
    return [value, got[1], got[3], got[2]]


def after(value, *earlier):
    return lax.optimization_barrier((value, *earlier))[0]


def sum_feat(first, images, pair, body, beside=None):
    got, sent, waits = {}, {}, ()
    for distance in ORDER:
        mine, other = first if distance == FIRST else images(distance, after(pair, *waits))
        other = exchange(other, HERE, 1)
        if distance:
            sent[distance] = mine + other
            got[distance] = exchange(sent[distance], HERE, 2 * distance)
        waits = {ORDER[1]: (sent[FIRST],), ORDER[2]: tuple(sent.values())}.get(distance, ())
    extra = None
    if beside is not None:
        extra = beside(mine)
        got[1], extra = lax.optimization_barrier((got[1], extra))
    tiles = (sent[FIRST][body:] + got[1][body:]) + (got[3][body:] + got[2][body:])
    return ((mine[0:body] + got[1][0:body]) + (got[3][0:body] + got[2][0:body])) + other[0:body], tiles, extra


def spread_feat(value, project):
    got = {d: exchange(value, HERE, 2 * d) if d else value for d in ORDER}
    far = {0: exchange(got[0], HERE, 1)}
    before = project(0, got[0], far[0], ())
    for d in (2, 3, 1):
        far[d] = exchange(after(got[d], *before), HERE, 1)
    for d in (2, 3, 1):
        before = project(d, got[d], far[d], before)
    return before


def local(features, targets, counts, ranks):
    slots, width = features.shape
    part = slots // XCHIPS
    body = part // LANES * HALF
    shape = jax.ShapeDtypeStruct
    summed = shape((width // LANES * K + TILE, LANES), f32)
    field_like, small = shape((K, width), f32), shape((K, K), f32)
    pair_like = shape((2 * K, width), bf16)
    share = 1.0 / XCHIPS

    def tiles_like(tiles):
        return shape((tiles * TILE, LANES), f32)

    def images_like(tiles):
        return [shape((body + tiles * TILE, LANES), f32)] * 2

    high, low, scale, out = call(
        k1,
        [pltpu.VMEM((slots, width), bf16), pltpu.VMEM((slots, width), bf16), shape((1, slots), f32), summed],
        (counts, in_hbm(ranks.reshape(1, slots)), in_hbm(targets), in_hbm(features)),
        [IN_SMEM, IN_HBM, IN_HBM, IN_HBM],
        (
            pltpu.VMEM((BUFFERS, STREAM, width), f32),
            pltpu.VMEM((K, slots), f32),
            pltpu.VMEM((1, slots), jnp.int32),
            pltpu.SemaphoreType.DMA((BUFFERS,)),
            pltpu.SemaphoreType.DMA((2,)),
        ),
        1.0,
    )

    def images(tiles):
        def of(distance, pair):
            count = tiles.shape[0] // TILE
            return call(images_at(distance), images_like(count), (pair, tiles, high, low), passes=share)

        return of

    parts = gather_rows(out)
    field, norm, pair, tiles, *first = call(
        k2,
        [field_like, tiles_like(1), pair_like, tiles_like(1), *images_like(1)],
        (*parts, high, low),
        passes=share,
    )
    own, tile_b, _ = sum_feat(first, images(tiles), pair, body)
    kept = {}

    def project(distance, near, far, before):
        out, kept[distance] = call(
            back_at(distance, not before),
            [summed, shape((K, part), f32)],
            (near, far, scale, high, low, *before),
            passes=share if before else share,
        )
        return (out,)

    parts = gather_rows(*spread_feat(own, project))
    applied, curve, pair, tiles, *first = call(
        k4,
        [field_like, tiles_like(1), pair_like, tiles_like(2), *images_like(2)],
        (*parts, field, norm, high, low),
        passes=share,
    )

    def begin(own_images):
        return call(first_step, [small], (after(curve, own_images), tile_b), passes=share)[0]

    own, tiles, step = sum_feat(first, images(tiles), pair, body, begin)
    mix, gram_new, cross = call(solve_coef, [shape((K, 2 * K), f32), small, small], (tile_b, tiles, step), passes=share)

    def mixed_project(distance, near, far, before):
        return call(
            mixed_back_at(distance, not before),
            [summed],
            (near, far, scale, high, low, mix, kept[distance], *before),
            passes=share,
        )

    parts = gather_rows(*spread_feat(own, mixed_project))
    ready = call(prepare, [field_like] * 3 + [small], (field, applied, tile_b, mix, gram_new, cross, step))
    return tuple(call(k6, [field_like, field_like], (*parts, norm, gram_new, *ready)))


def solution(mesh):
    placed = (P("rows", "feat"), P(None, "rows"), P("rows"), P("rows"))
    return jax.shard_map(
        local,
        mesh=mesh,
        in_specs=placed,
        out_specs=(P(None, "feat"), P(None, "feat")),
        check_vma=False,
    )
```

```python
import jax
import jax.numpy as jnp
from jax import lax
from jax.experimental import pallas as pl
from jax.experimental.pallas import tpu as pltpu
from jax.sharding import PartitionSpec as P


K = 32
HALF = K // 2
LANES = 128
TILE = 8
XCHIPS = 4
ORDER = (2, 3, 1, 0)
FIRST = ORDER[0]
HERE = (0, 0)
CHUNK = 1024
STREAM = 256
BUFFERS = 8
prio_power = 0.7
weight_power = 0.5
ridge_shift = 0.5
f32, bf16 = jnp.float32, jnp.bfloat16
IN_VMEM = pl.BlockSpec(memory_space=pltpu.VMEM)
IN_SMEM = pl.BlockSpec(memory_space=pltpu.SMEM)
IN_HBM = pl.BlockSpec(memory_space=pltpu.HBM)
ROWS_BY_ROWS = (((1,), (1,)), ((), ()))


def split(value):
    high = value.astype(bf16)
    return high, (value - high.astype(f32)).astype(bf16)


def exact(left, right):
    return jnp.dot(left, right, precision=lax.Precision.HIGHEST, preferred_element_type=f32)


def row_gram(left, right):
    return lax.dot_general(left, right, ROWS_BY_ROWS, precision=lax.Precision.HIGHEST, preferred_element_type=f32)


def solve_t(matrix, rhs_block):
    matrix = 0.5 * (matrix + matrix.T)
    table = jnp.concatenate([matrix, rhs_block], axis=1)
    for k in range(0, K, TILE):
        columns = [jnp.broadcast_to(table[:, k + j : k + j + 1], table.shape) for j in range(TILE)]
        rows = [table[k + i : k + i + 1, :] for i in range(TILE)]
        pivot = [[column[k + i : k + i + 1, :] for column in columns] for i in range(TILE)]
        for p in range(TILE):
            inverse = 1.0 / pivot[p][p]
            rows[p] = rows[p] * inverse
            pivot[p] = [value * inverse for value in pivot[p]]
            for i in range(TILE):
                if i != p:
                    factor = pivot[i][p]
                    rows[i] = rows[i] - factor * rows[p]
                    for j in range(p + 1, TILE):
                        pivot[i][j] = pivot[i][j] - factor * pivot[p][j]
        change = columns[0] * rows[0]
        for j in range(1, TILE):
            change = change + columns[j] * rows[j]
        table = table - change
        pieces = [table[0:k], *rows, table[k + TILE :]]
        table = jnp.concatenate([piece for piece in pieces if piece.shape[0]], axis=0)
    return table[:, K:].T


def merged(parts):
    a, b, c, d = (part[...] for part in parts)
    return (a + b) + (c + d)


def pack(square):
    return jnp.concatenate([square[i : i + TILE] for i in range(0, K, TILE)], axis=1)


def unpack(tile):
    return jnp.concatenate([tile[:, i : i + K] for i in range(0, LANES, K)], axis=0)


def put_blocks(out, value, tile):
    blocks = value.shape[1] // LANES
    for j in range(blocks):
        out[j * K : (j + 1) * K, :] = value[:, j * LANES : (j + 1) * LANES]
    out[blocks * K :, :] = tile


def get_blocks(stacked):
    blocks = stacked.shape[0] // K
    value = jnp.concatenate([stacked[j * K : (j + 1) * K] for j in range(blocks)], axis=1)
    return value, stacked[blocks * K :]


def k1(count, ranks_hbm, targets_hbm, features, high, low, scale, out, buf, targets, ranks, sem, in_sem):
    slots, width = features.shape
    steps = slots // STREAM
    small = [
        pltpu.make_async_copy(ranks_hbm, ranks, in_sem.at[0]),
        pltpu.make_async_copy(targets_hbm, targets, in_sem.at[1]),
    ]
    copies = [
        pltpu.make_async_copy(features.at[pl.ds(c * STREAM, STREAM)], buf.at[c % BUFFERS], sem.at[c % BUFFERS])
        for c in range(steps)
    ]
    for copy in small:
        copy.start()
    for c in range(BUFFERS):
        copies[c].start()
    live = lax.broadcasted_iota(jnp.int32, (1, slots), 1) < count[0]
    small[0].wait()
    log_rank = jnp.log(ranks[...].astype(f32))
    scale_now = jnp.where(live, jnp.exp((prio_power * weight_power) * log_rank), 0.0)
    scale[...] = scale_now
    prio_sum = jnp.sum(jnp.where(live, jnp.exp(-prio_power * log_rank), 0.0))
    small[1].wait()
    total = jnp.zeros((2 * K, width), f32)
    rest = jnp.zeros((K, width), f32)
    for c in range(steps):
        at = slice(c * STREAM, (c + 1) * STREAM)
        high_t, low_t = split(targets[:, at] * scale_now[:, at])
        copies[c].wait()
        high_f, low_f = split(buf[c % BUFFERS])
        if c + BUFFERS < steps:
            copies[c + BUFFERS].start()
        high[at, :] = high_f
        low[at, :] = low_f
        total += jnp.dot(jnp.concatenate([high_t, low_t], axis=0), high_f, preferred_element_type=f32)
        rest += jnp.dot(high_t, low_f, preferred_element_type=f32)
    row = lax.broadcasted_iota(jnp.int32, (TILE, LANES), 0)
    col = lax.broadcasted_iota(jnp.int32, (TILE, LANES), 1)
    tail = jnp.where(col == 0, prio_sum, jnp.where(col == 1, count[0].astype(f32), 0.0))
    put_blocks(out, total[0:K] + total[K:] + rest, jnp.where(row == 0, tail, 0.0))


def put_images(distance, pair, tiles, high, low, mine, other):
    place = lax.axis_index("feat")
    x, first = place // 2, place % 2 == 0
    part = high.shape[0] // XCHIPS
    base = pl.multiple_of((x ^ distance) * part, part)
    for piece in range(0, part, CHUNK):
        at = pl.ds(pl.multiple_of(base + piece, CHUNK), CHUNK)
        both = lax.dot_general(pair, high[at, :], ROWS_BY_ROWS, preferred_element_type=f32)
        rest = lax.dot_general(pair[0:K], low[at, :], ROWS_BY_ROWS, preferred_element_type=f32)
        value = both[0:K] + both[K:] + rest
        here = jnp.where(first, value[0:HALF], value[HALF:])
        there = jnp.where(first, value[HALF:], value[0:HALF])
        for j in range(0, CHUNK, LANES):
            to = (piece + j) // LANES * HALF
            mine[to : to + HALF, :] = here[:, j : j + LANES]
            other[to : to + HALF, :] = there[:, j : j + LANES]
    mine[part // LANES * HALF :, :] = tiles
    other[part // LANES * HALF :, :] = tiles


def put_pair(value, pair):
    high_v, low_v = split(value)
    pair[0:K, :] = high_v
    pair[K:, :] = low_v


def k2(p0, p1, p2, p3, high, low, field, norm, pair, tiles, mine, other):
    total, tile = get_blocks(merged((p0, p1, p2, p3)))
    factor = jnp.sqrt(tile[0:1, 0:1] / tile[0:1, 1:2])
    norm[...] = jnp.broadcast_to(factor, norm.shape)
    rhs_field = total * factor
    field[...] = rhs_field
    put_pair(rhs_field, pair)
    tiles[...] = pack(row_gram(rhs_field, rhs_field))
    put_images(FIRST, pair[...], tiles[...], high, low, mine, other)


def images_at(distance):
    def images_kernel(pair, tiles, high, low, mine, other):
        put_images(distance, pair[...], tiles[...], high, low, mine, other)

    return images_kernel


def get_images(near, far):
    first = lax.axis_index("feat") % 2 == 0
    blocks = []
    for at in range(0, near.shape[0], HALF):
        a, b = near[at : at + HALF, :], far[at : at + HALF, :]
        blocks.append(jnp.concatenate([jnp.where(first, a, b), jnp.where(first, b, a)], axis=0))
    return jnp.concatenate(blocks, axis=1)


def back_project(distance, images, scale, high, low, before, out):
    x = lax.axis_index("feat") // 2
    part, width = images.shape[1], high.shape[1]
    total = jnp.zeros((2 * K, width), f32)
    rest = jnp.zeros((K, width), f32)
    base = pl.multiple_of((x ^ distance) * part, part)
    high_w, low_w = split(images * scale[:, pl.ds(base, part)])
    pair = jnp.concatenate([high_w, low_w], axis=0)
    curve = lax.dot_general(pair, jnp.concatenate(split(images), axis=0), ROWS_BY_ROWS, preferred_element_type=f32)
    for piece in range(0, part, CHUNK):
        at = pl.ds(pl.multiple_of(base + piece, CHUNK), CHUNK)
        to = slice(piece, piece + CHUNK)
        total += jnp.dot(pair[:, to], high[at, :], preferred_element_type=f32)
        rest += jnp.dot(high_w[:, to], low[at, :], preferred_element_type=f32)
    value = total[0:K] + total[K:] + rest
    tile = pack(curve[0:K, 0:K] + curve[0:K, K:] + curve[K:, 0:K])
    if before is not None:
        value_before, tile_before = get_blocks(before[...])
        value, tile = value_before + value, tile_before + tile
    put_blocks(out, value, tile)


def back_at(distance, begins):
    def back_kernel(near, far, scale, high, low, *rest):
        before, (out, kept) = (None, rest) if begins else (rest[0], rest[1:])
        images = get_images(near, far)
        kept[...] = images
        back_project(distance, images, scale, high, low, before, out)

    return back_kernel


def mixed_back_at(distance, begins):
    def mixed_back_kernel(near, far, scale, high, low, mix, kept, *rest):
        before, (out,) = (None, rest) if begins else (rest[0], rest[1:])
        was = kept[...]
        images = was + exact(mix[...], jnp.concatenate([was, get_images(near, far)], axis=0))
        back_project(distance, images, scale, high, low, before, out)

    return mixed_back_kernel


def k4(z0, z1, z2, z3, field, norm, high, low, applied, curve, pair, tiles, mine, other):
    total, tile = get_blocks(merged((z0, z1, z2, z3)))
    factor = norm[0:1, 0:1]
    curve[...] = tile * factor
    backward = total * factor + ridge_shift * field[...]
    applied[...] = backward
    put_pair(backward, pair)
    tiles[0:TILE, :] = pack(row_gram(backward, backward))
    tiles[TILE:, :] = pack(row_gram(backward, field[...]))
    put_images(FIRST, pair[...], tiles[...], high, low, mine, other)


def first_step(curve, tile_b, step):
    gram = unpack(tile_b[...])
    step[...] = solve_t(unpack(curve[...]) + ridge_shift * gram, gram)


def solve_coef(tile_b, tiles, step, mix, gram_new, cross):
    gram, step_t = unpack(tile_b[...]), step[...]
    moved = exact(step_t, unpack(tiles[TILE:, :]))
    square = gram - moved - moved.T + row_gram(exact(step_t, unpack(tiles[0:TILE, :])), step_t)
    gram_new[...] = square
    cross[...] = gram - moved
    mix[...] = jnp.concatenate([solve_t(gram, square), -step_t], axis=1)


def prepare(field, applied, tile_b, mix, gram_new, cross, step, residual, begun, direction, square):
    coef_t = mix[:, 0:K]
    mixed = row_gram(cross[...], coef_t)
    square[...] = gram_new[...] + mixed + mixed.T + row_gram(exact(coef_t, unpack(tile_b[...])), coef_t)
    now = field[...] - exact(step[...], applied[...])
    residual[...] = now
    direction[...] = now + exact(coef_t, field[...])
    begun[...] = exact(step[...], field[...])


def k6(z0, z1, z2, z3, norm, gram_new, residual, begun, direction, square, solution_out, residual_out):
    total, tile = get_blocks(merged((z0, z1, z2, z3)))
    factor = norm[0:1, 0:1]
    curvature = unpack(tile) * factor + ridge_shift * square[...]
    step_t = solve_t(curvature, gram_new[...])
    backward = total * factor + ridge_shift * direction[...]
    solution_out[...] = begun[...] + exact(step_t, direction[...])
    residual_out[...] = residual[...] - exact(step_t, backward)


def call(kernel, outs, operands, specs=None, scratch=(), passes=0.0):
    cost = pl.CostEstimate(
        flops=int(passes * 3 * 2 * K * 4096 * 1024), bytes_accessed=int(passes * (1 << 24)), transcendentals=0
    )
    return pl.pallas_call(
        kernel,
        out_shape=outs,
        in_specs=specs or [IN_VMEM] * len(operands),
        out_specs=[IN_VMEM] * len(outs),
        scratch_shapes=scratch,
        compiler_params=pltpu.CompilerParams(vmem_limit_bytes=24 << 20),
        cost_estimate=cost,
        name=kernel.__name__,
    )(*operands)


def in_hbm(value):
    return pltpu.with_memory_space_constraint(value, pltpu.HBM)


def exchange(value, row_distance, feat_distance):
    pairs = [
        (r * 8 + f, (r ^ row_distance[f % 2]) * 8 + (f ^ feat_distance)) for r in range(16) for f in range(8)
    ]
    return lax.ppermute(value, ("rows", "feat"), pairs)


def gather_rows(value):
    got = {d: exchange(value, (d, 4 * d), 0) for d in (1, 3, 2)}
    value = (value + got[1]) + (got[3] + got[2])
    got = {d: exchange(value, (4 * d, d), 0) for d in (1, 3, 2)}
    return [value, got[1], got[3], got[2]]


def after(value, *earlier):
    return lax.optimization_barrier((value, *earlier))[0]


def sum_feat(first, images, pair, body, beside=None):
    got, sent, waits = {}, {}, ()
    for distance in ORDER:
        mine, other = first if distance == FIRST else images(distance, after(pair, *waits))
        other = exchange(other, HERE, 1)
        if distance:
            sent[distance] = mine + other
            got[distance] = exchange(sent[distance], HERE, 2 * distance)
        waits = {ORDER[1]: (sent[FIRST],), ORDER[2]: tuple(sent.values())}.get(distance, ())
    extra = None
    if beside is not None:
        extra = beside(mine)
        got[1], extra = lax.optimization_barrier((got[1], extra))
    tiles = (sent[FIRST][body:] + got[1][body:]) + (got[3][body:] + got[2][body:])
    return ((mine[0:body] + got[1][0:body]) + (got[3][0:body] + got[2][0:body])) + other[0:body], tiles, extra


def spread_feat(value, project):
    got = {d: exchange(value, HERE, 2 * d) if d else value for d in ORDER}
    far = {0: exchange(got[0], HERE, 1)}
    before = project(0, got[0], far[0], ())
    for d in (2, 3, 1):
        far[d] = exchange(after(got[d], *before), HERE, 1)
    for d in (2, 3, 1):
        before = project(d, got[d], far[d], before)
    return before


def local(features, targets, counts, ranks):
    slots, width = features.shape
    part = slots // XCHIPS
    body = part // LANES * HALF
    shape = jax.ShapeDtypeStruct
    summed = shape((width // LANES * K + TILE, LANES), f32)
    field_like, small = shape((K, width), f32), shape((K, K), f32)
    pair_like = shape((2 * K, width), bf16)
    share = 1.0 / XCHIPS

    def tiles_like(tiles):
        return shape((tiles * TILE, LANES), f32)

    def images_like(tiles):
        return [shape((body + tiles * TILE, LANES), f32)] * 2

    high, low, scale, out = call(
        k1,
        [pltpu.VMEM((slots, width), bf16), pltpu.VMEM((slots, width), bf16), shape((1, slots), f32), summed],
        (counts, in_hbm(ranks.reshape(1, slots)), in_hbm(targets), in_hbm(features)),
        [IN_SMEM, IN_HBM, IN_HBM, IN_HBM],
        (
            pltpu.VMEM((BUFFERS, STREAM, width), f32),
            pltpu.VMEM((K, slots), f32),
            pltpu.VMEM((1, slots), jnp.int32),
            pltpu.SemaphoreType.DMA((BUFFERS,)),
            pltpu.SemaphoreType.DMA((2,)),
        ),
        1.0,
    )

    def images(tiles):
        def of(distance, pair):
            count = tiles.shape[0] // TILE
            return call(images_at(distance), images_like(count), (pair, tiles, high, low), passes=share)

        return of

    parts = gather_rows(out)
    field, norm, pair, tiles, *first = call(
        k2,
        [field_like, tiles_like(1), pair_like, tiles_like(1), *images_like(1)],
        (*parts, high, low),
        passes=share,
    )
    own, tile_b, _ = sum_feat(first, images(tiles), pair, body)
    kept = {}

    def project(distance, near, far, before):
        out, kept[distance] = call(
            back_at(distance, not before),
            [summed, shape((K, part), f32)],
            (near, far, scale, high, low, *before),
            passes=share if before else share,
        )
        return (out,)

    parts = gather_rows(*spread_feat(own, project))
    applied, curve, pair, tiles, *first = call(
        k4,
        [field_like, tiles_like(1), pair_like, tiles_like(2), *images_like(2)],
        (*parts, field, norm, high, low),
        passes=share,
    )

    def begin(own_images):
        return call(first_step, [small], (after(curve, own_images), tile_b), passes=share)[0]

    own, tiles, step = sum_feat(first, images(tiles), pair, body, begin)
    mix, gram_new, cross = call(solve_coef, [shape((K, 2 * K), f32), small, small], (tile_b, tiles, step), passes=share)

    def mixed_project(distance, near, far, before):
        return call(
            mixed_back_at(distance, not before),
            [summed],
            (near, far, scale, high, low, mix, kept[distance], *before),
            passes=share,
        )

    parts = gather_rows(*spread_feat(own, mixed_project))
    ready = call(prepare, [field_like] * 3 + [small], (field, applied, tile_b, mix, gram_new, cross, step))
    return tuple(call(k6, [field_like, field_like], (*parts, norm, gram_new, *ready)))


def solution(mesh):
    placed = (P("rows", "feat"), P(None, "rows"), P("rows"), P("rows"))
    return jax.shard_map(
        local,
        mesh=mesh,
        in_specs=placed,
        out_specs=(P(None, "feat"), P(None, "feat")),
        check_vma=False,
    )
```

```python
import jax
import jax.numpy as jnp
from jax import lax
from jax.experimental import pallas as pl
from jax.experimental.pallas import tpu as pltpu
from jax.sharding import PartitionSpec as P


K = 32
HALF = K // 2
LANES = 128
TILE = 8
XCHIPS = 4
ORDER = (2, 3, 1, 0)
FIRST = ORDER[0]
HERE = (0, 0)
CHUNK = 1024
STREAM = 256
BUFFERS = 6
prio_power = 0.7
weight_power = 0.5
ridge_shift = 0.5
f32, bf16 = jnp.float32, jnp.bfloat16
IN_VMEM = pl.BlockSpec(memory_space=pltpu.VMEM)
IN_SMEM = pl.BlockSpec(memory_space=pltpu.SMEM)
IN_HBM = pl.BlockSpec(memory_space=pltpu.HBM)
ROWS_BY_ROWS = (((1,), (1,)), ((), ()))


def split(value):
    high = value.astype(bf16)
    return high, (value - high.astype(f32)).astype(bf16)


def exact(left, right):
    return jnp.dot(left, right, precision=lax.Precision.HIGHEST, preferred_element_type=f32)


def row_gram(left, right):
    return lax.dot_general(left, right, ROWS_BY_ROWS, precision=lax.Precision.HIGHEST, preferred_element_type=f32)


def solve_t(matrix, rhs_block):
    matrix = 0.5 * (matrix + matrix.T)
    table = jnp.concatenate([matrix, rhs_block], axis=1)
    for k in range(0, K, TILE):
        columns = [jnp.broadcast_to(table[:, k + j : k + j + 1], table.shape) for j in range(TILE)]
        rows = [table[k + i : k + i + 1, :] for i in range(TILE)]
        pivot = [[column[k + i : k + i + 1, :] for column in columns] for i in range(TILE)]
        for p in range(TILE):
            inverse = 1.0 / pivot[p][p]
            rows[p] = rows[p] * inverse
            pivot[p] = [value * inverse for value in pivot[p]]
            for i in range(TILE):
                if i != p:
                    factor = pivot[i][p]
                    rows[i] = rows[i] - factor * rows[p]
                    for j in range(p + 1, TILE):
                        pivot[i][j] = pivot[i][j] - factor * pivot[p][j]
        change = columns[0] * rows[0]
        for j in range(1, TILE):
            change = change + columns[j] * rows[j]
        table = table - change
        pieces = [table[0:k], *rows, table[k + TILE :]]
        table = jnp.concatenate([piece for piece in pieces if piece.shape[0]], axis=0)
    return table[:, K:].T


def merged(parts):
    a, b, c, d = (part[...] for part in parts)
    return (a + b) + (c + d)


def pack(square):
    return jnp.concatenate([square[i : i + TILE] for i in range(0, K, TILE)], axis=1)


def unpack(tile):
    return jnp.concatenate([tile[:, i : i + K] for i in range(0, LANES, K)], axis=0)


def put_blocks(out, value, tile):
    blocks = value.shape[1] // LANES
    for j in range(blocks):
        out[j * K : (j + 1) * K, :] = value[:, j * LANES : (j + 1) * LANES]
    out[blocks * K :, :] = tile


def get_blocks(stacked):
    blocks = stacked.shape[0] // K
    value = jnp.concatenate([stacked[j * K : (j + 1) * K] for j in range(blocks)], axis=1)
    return value, stacked[blocks * K :]


def k1(count, ranks_hbm, targets_hbm, features, high, low, scale, out, buf, targets, ranks, sem, in_sem):
    slots, width = features.shape
    steps = slots // STREAM
    small = [
        pltpu.make_async_copy(ranks_hbm, ranks, in_sem.at[0]),
        pltpu.make_async_copy(targets_hbm, targets, in_sem.at[1]),
    ]
    copies = [
        pltpu.make_async_copy(features.at[pl.ds(c * STREAM, STREAM)], buf.at[c % BUFFERS], sem.at[c % BUFFERS])
        for c in range(steps)
    ]
    small[0].start()
    copies[0].start()
    small[1].start()
    for c in range(1, BUFFERS):
        copies[c].start()
    live = lax.broadcasted_iota(jnp.int32, (1, slots), 1) < count[0]
    small[0].wait()
    log_rank = jnp.log(ranks[...].astype(f32))
    scale_now = jnp.where(live, jnp.exp((prio_power * weight_power) * log_rank), 0.0)
    scale[...] = scale_now
    prio_sum = jnp.sum(jnp.where(live, jnp.exp(-prio_power * log_rank), 0.0))
    small[1].wait()
    total = jnp.zeros((2 * K, width), f32)
    rest = jnp.zeros((K, width), f32)
    for c in range(steps):
        at = slice(c * STREAM, (c + 1) * STREAM)
        high_t, low_t = split(targets[:, at] * scale_now[:, at])
        copies[c].wait()
        high_f, low_f = split(buf[c % BUFFERS])
        if c + BUFFERS < steps:
            copies[c + BUFFERS].start()
        high[at, :] = high_f
        low[at, :] = low_f
        total += jnp.dot(jnp.concatenate([high_t, low_t], axis=0), high_f, preferred_element_type=f32)
        rest += jnp.dot(high_t, low_f, preferred_element_type=f32)
    row = lax.broadcasted_iota(jnp.int32, (TILE, LANES), 0)
    col = lax.broadcasted_iota(jnp.int32, (TILE, LANES), 1)
    tail = jnp.where(col == 0, prio_sum, jnp.where(col == 1, count[0].astype(f32), 0.0))
    put_blocks(out, total[0:K] + total[K:] + rest, jnp.where(row == 0, tail, 0.0))


def put_images(distance, pair, tiles, high, low, mine, other):
    place = lax.axis_index("feat")
    x, first = place // 2, place % 2 == 0
    part = high.shape[0] // XCHIPS
    base = pl.multiple_of((x ^ distance) * part, part)
    for piece in range(0, part, CHUNK):
        at = pl.ds(pl.multiple_of(base + piece, CHUNK), CHUNK)
        both = lax.dot_general(pair, high[at, :], ROWS_BY_ROWS, preferred_element_type=f32)
        rest = lax.dot_general(pair[0:K], low[at, :], ROWS_BY_ROWS, preferred_element_type=f32)
        value = both[0:K] + both[K:] + rest
        here = jnp.where(first, value[0:HALF], value[HALF:])
        there = jnp.where(first, value[HALF:], value[0:HALF])
        for j in range(0, CHUNK, LANES):
            to = (piece + j) // LANES * HALF
            mine[to : to + HALF, :] = here[:, j : j + LANES]
            other[to : to + HALF, :] = there[:, j : j + LANES]
    mine[part // LANES * HALF :, :] = tiles
    other[part // LANES * HALF :, :] = tiles


def put_pair(value, pair):
    high_v, low_v = split(value)
    pair[0:K, :] = high_v
    pair[K:, :] = low_v


def k2(p0, p1, p2, p3, high, low, field, norm, pair, tiles, mine, other):
    total, tile = get_blocks(merged((p0, p1, p2, p3)))
    factor = jnp.sqrt(tile[0:1, 0:1] / tile[0:1, 1:2])
    norm[...] = jnp.broadcast_to(factor, norm.shape)
    rhs_field = total * factor
    field[...] = rhs_field
    put_pair(rhs_field, pair)
    tiles[...] = pack(row_gram(rhs_field, rhs_field))
    put_images(FIRST, pair[...], tiles[...], high, low, mine, other)


def images_at(distance):
    def images_kernel(pair, tiles, high, low, mine, other):
        put_images(distance, pair[...], tiles[...], high, low, mine, other)

    return images_kernel


def get_images(near, far):
    first = lax.axis_index("feat") % 2 == 0
    blocks = []
    for at in range(0, near.shape[0], HALF):
        a, b = near[at : at + HALF, :], far[at : at + HALF, :]
        blocks.append(jnp.concatenate([jnp.where(first, a, b), jnp.where(first, b, a)], axis=0))
    return jnp.concatenate(blocks, axis=1)


def back_project(distance, images, scale, high, low, before, out):
    x = lax.axis_index("feat") // 2
    part, width = images.shape[1], high.shape[1]
    total = jnp.zeros((2 * K, width), f32)
    rest = jnp.zeros((K, width), f32)
    base = pl.multiple_of((x ^ distance) * part, part)
    high_w, low_w = split(images * scale[:, pl.ds(base, part)])
    pair = jnp.concatenate([high_w, low_w], axis=0)
    curve = lax.dot_general(pair, jnp.concatenate(split(images), axis=0), ROWS_BY_ROWS, preferred_element_type=f32)
    for piece in range(0, part, CHUNK):
        at = pl.ds(pl.multiple_of(base + piece, CHUNK), CHUNK)
        to = slice(piece, piece + CHUNK)
        total += jnp.dot(pair[:, to], high[at, :], preferred_element_type=f32)
        rest += jnp.dot(high_w[:, to], low[at, :], preferred_element_type=f32)
    value = total[0:K] + total[K:] + rest
    tile = pack(curve[0:K, 0:K] + curve[0:K, K:] + curve[K:, 0:K])
    if before is not None:
        value_before, tile_before = get_blocks(before[...])
        value, tile = value_before + value, tile_before + tile
    put_blocks(out, value, tile)


def back_at(distance, begins):
    def back_kernel(near, far, scale, high, low, *rest):
        before, (out, kept) = (None, rest) if begins else (rest[0], rest[1:])
        images = get_images(near, far)
        kept[...] = images
        back_project(distance, images, scale, high, low, before, out)

    return back_kernel


def mixed_back_at(distance, begins):
    def mixed_back_kernel(near, far, scale, high, low, mix, kept, *rest):
        before, (out,) = (None, rest) if begins else (rest[0], rest[1:])
        was = kept[...]
        images = was + exact(mix[...], jnp.concatenate([was, get_images(near, far)], axis=0))
        back_project(distance, images, scale, high, low, before, out)

    return mixed_back_kernel


def k4(z0, z1, z2, z3, field, norm, high, low, applied, curve, pair, tiles, mine, other):
    total, tile = get_blocks(merged((z0, z1, z2, z3)))
    factor = norm[0:1, 0:1]
    curve[...] = tile * factor
    backward = total * factor + ridge_shift * field[...]
    applied[...] = backward
    put_pair(backward, pair)
    tiles[0:TILE, :] = pack(row_gram(backward, backward))
    tiles[TILE:, :] = pack(row_gram(backward, field[...]))
    put_images(FIRST, pair[...], tiles[...], high, low, mine, other)


def first_step(curve, tile_b, step):
    gram = unpack(tile_b[...])
    step[...] = solve_t(unpack(curve[...]) + ridge_shift * gram, gram)


def solve_coef(tile_b, tiles, step, mix, gram_new, cross):
    gram, step_t = unpack(tile_b[...]), step[...]
    moved = exact(step_t, unpack(tiles[TILE:, :]))
    square = gram - moved - moved.T + row_gram(exact(step_t, unpack(tiles[0:TILE, :])), step_t)
    gram_new[...] = square
    cross[...] = gram - moved
    mix[...] = jnp.concatenate([solve_t(gram, square), -step_t], axis=1)


def prepare(field, applied, tile_b, mix, gram_new, cross, step, residual, begun, direction, square):
    coef_t = mix[:, 0:K]
    mixed = row_gram(cross[...], coef_t)
    square[...] = gram_new[...] + mixed + mixed.T + row_gram(exact(coef_t, unpack(tile_b[...])), coef_t)
    now = field[...] - exact(step[...], applied[...])
    residual[...] = now
    direction[...] = now + exact(coef_t, field[...])
    begun[...] = exact(step[...], field[...])


def k6(z0, z1, z2, z3, norm, gram_new, residual, begun, direction, square, solution_out, residual_out):
    total, tile = get_blocks(merged((z0, z1, z2, z3)))
    factor = norm[0:1, 0:1]
    curvature = unpack(tile) * factor + ridge_shift * square[...]
    step_t = solve_t(curvature, gram_new[...])
    backward = total * factor + ridge_shift * direction[...]
    solution_out[...] = begun[...] + exact(step_t, direction[...])
    residual_out[...] = residual[...] - exact(step_t, backward)


def call(kernel, outs, operands, specs=None, scratch=(), passes=0.0):
    cost = pl.CostEstimate(
        flops=int(passes * 3 * 2 * K * 4096 * 1024), bytes_accessed=int(passes * (1 << 24)), transcendentals=0
    )
    return pl.pallas_call(
        kernel,
        out_shape=outs,
        in_specs=specs or [IN_VMEM] * len(operands),
        out_specs=[IN_VMEM] * len(outs),
        scratch_shapes=scratch,
        compiler_params=pltpu.CompilerParams(vmem_limit_bytes=24 << 20),
        cost_estimate=cost,
        name=kernel.__name__,
    )(*operands)


def in_hbm(value):
    return pltpu.with_memory_space_constraint(value, pltpu.HBM)


def exchange(value, row_distance, feat_distance):
    pairs = [
        (r * 8 + f, (r ^ row_distance[f % 2]) * 8 + (f ^ feat_distance)) for r in range(16) for f in range(8)
    ]
    return lax.ppermute(value, ("rows", "feat"), pairs)


def gather_rows(value):
    got = {d: exchange(value, (d, 4 * d), 0) for d in (1, 3, 2)}
    value = (value + got[1]) + (got[3] + got[2])
    got = {d: exchange(value, (4 * d, d), 0) for d in (1, 3, 2)}
    return [value, got[1], got[3], got[2]]


def after(value, *earlier):
    return lax.optimization_barrier((value, *earlier))[0]


def sum_feat(first, images, pair, body, beside=None):
    got, sent, waits = {}, {}, ()
    for distance in ORDER:
        mine, other = first if distance == FIRST else images(distance, after(pair, *waits))
        other = exchange(other, HERE, 1)
        if distance:
            sent[distance] = mine + other
            got[distance] = exchange(sent[distance], HERE, 2 * distance)
        waits = {ORDER[1]: (sent[FIRST],), ORDER[2]: tuple(sent.values())}.get(distance, ())
    extra = None
    if beside is not None:
        extra = beside(mine)
        got[1], extra = lax.optimization_barrier((got[1], extra))
    tiles = (sent[FIRST][body:] + got[1][body:]) + (got[3][body:] + got[2][body:])
    return ((mine[0:body] + got[1][0:body]) + (got[3][0:body] + got[2][0:body])) + other[0:body], tiles, extra


def spread_feat(value, project):
    got = {d: exchange(value, HERE, 2 * d) if d else value for d in ORDER}
    far = {0: exchange(got[0], HERE, 1)}
    before = project(0, got[0], far[0], ())
    for d in (2, 3, 1):
        far[d] = exchange(after(got[d], *before), HERE, 1)
    for d in (2, 3, 1):
        before = project(d, got[d], far[d], before)
    return before


def local(features, targets, counts, ranks):
    slots, width = features.shape
    part = slots // XCHIPS
    body = part // LANES * HALF
    shape = jax.ShapeDtypeStruct
    summed = shape((width // LANES * K + TILE, LANES), f32)
    field_like, small = shape((K, width), f32), shape((K, K), f32)
    pair_like = shape((2 * K, width), bf16)
    share = 1.0 / XCHIPS

    def tiles_like(tiles):
        return shape((tiles * TILE, LANES), f32)

    def images_like(tiles):
        return [shape((body + tiles * TILE, LANES), f32)] * 2

    high, low, scale, out = call(
        k1,
        [pltpu.VMEM((slots, width), bf16), pltpu.VMEM((slots, width), bf16), shape((1, slots), f32), summed],
        (counts, in_hbm(ranks.reshape(1, slots)), in_hbm(targets), in_hbm(features)),
        [IN_SMEM, IN_HBM, IN_HBM, IN_HBM],
        (
            pltpu.VMEM((BUFFERS, STREAM, width), f32),
            pltpu.VMEM((K, slots), f32),
            pltpu.VMEM((1, slots), jnp.int32),
            pltpu.SemaphoreType.DMA((BUFFERS,)),
            pltpu.SemaphoreType.DMA((2,)),
        ),
        1.0,
    )

    def images(tiles):
        def of(distance, pair):
            count = tiles.shape[0] // TILE
            return call(images_at(distance), images_like(count), (pair, tiles, high, low), passes=share)

        return of

    parts = gather_rows(out)
    field, norm, pair, tiles, *first = call(
        k2,
        [field_like, tiles_like(1), pair_like, tiles_like(1), *images_like(1)],
        (*parts, high, low),
        passes=share,
    )
    own, tile_b, _ = sum_feat(first, images(tiles), pair, body)
    kept = {}

    def project(distance, near, far, before):
        out, kept[distance] = call(
            back_at(distance, not before),
            [summed, shape((K, part), f32)],
            (near, far, scale, high, low, *before),
            passes=share if before else share,
        )
        return (out,)

    parts = gather_rows(*spread_feat(own, project))
    applied, curve, pair, tiles, *first = call(
        k4,
        [field_like, tiles_like(1), pair_like, tiles_like(2), *images_like(2)],
        (*parts, field, norm, high, low),
        passes=share,
    )

    def begin(own_images):
        return call(first_step, [small], (after(curve, own_images), tile_b), passes=share)[0]

    own, tiles, step = sum_feat(first, images(tiles), pair, body, begin)
    mix, gram_new, cross = call(solve_coef, [shape((K, 2 * K), f32), small, small], (tile_b, tiles, step), passes=share)

    def mixed_project(distance, near, far, before):
        return call(
            mixed_back_at(distance, not before),
            [summed],
            (near, far, scale, high, low, mix, kept[distance], *before),
            passes=share,
        )

    parts = gather_rows(*spread_feat(own, mixed_project))
    ready = call(prepare, [field_like] * 3 + [small], (field, applied, tile_b, mix, gram_new, cross, step))
    return tuple(call(k6, [field_like, field_like], (*parts, norm, gram_new, *ready)))


def solution(mesh):
    placed = (P("rows", "feat"), P(None, "rows"), P("rows"), P("rows"))
    return jax.shard_map(
        local,
        mesh=mesh,
        in_specs=placed,
        out_specs=(P(None, "feat"), P(None, "feat")),
        check_vma=False,
    )
```
